512 devices in a mesh: region: 32 (over x, z), mp: 16 (over y, core).
Axes of the slice: x: 4, y: 8, z: 8, core: 2. Of those that a mesh axis runs over, the one named last changes fastest.
Arguments:
- tokens: bfloat16 [32768, 1024], P('region', 'mp'), may hold values from -6 to 6
- cotangent: bfloat16 [32768, 1024], P('region', 'mp'), may hold values from -6 to 6
- gain: float32 [1024], replicated, may hold values from 0.1 to 1.9
- w_up: bfloat16 [1024, 4096], P(None, 'mp'), may hold values from -0.1875 to 0.1875
- w_down: bfloat16 [4096, 1024], P('mp'), may hold values from -0.09375 to 0.09375
- counts: int32 [128], P('region'), may hold values from 16 to 256, as said below
Outputs:
- d_tokens: bfloat16 [32768, 1024], P('region', 'mp')
- d_up: float32 [1024, 4096], P('region', 'mp')
- d_down: float32 [4096, 1024], P('mp', 'region')
- d_gain: float32 [1024], P('mp')
The draws below stay inside these ranges and needn't reach their ends.
Inputs may be any that keep to these rules, and one draw needn't show every extreme that they name: `counts`: each count is 16 times 1 + 3k for a whole k. Every group of 16 consecutive regions holds 1984 tokens, so all regions hold 15872 tokens together. The 4 regions of one owner hold at most 1024 tokens, and some owner holds exactly 1024 in every draw.
All inputs are finite; a program needn't handle non-finite values.
Results may differ from the reference program's by a relative error of at most 0.015.
Values may be sent and summed in bfloat16 or wider, within the bound.
A program may use at most 64 MiB of HBM per device.

```python
import math
import jax
import jax.numpy as jnp
from jax import lax

D = 1024
FF = 4096
TILE = 16
REG_DEV = 4
CAP = 1024
BAL = 496
REGIONS = 128
TOTAL = 15872
N_REGION = 32
N_MP = 16


def one_order(subkey):
    return jax.random.permutation(subkey, 16)


def draw_counts(key, part):
    groups = REGIONS // 16
    subkeys = jax.random.split(jax.random.fold_in(key, 11), groups)
    orders = jax.vmap(one_order)(subkeys)
    inverse = jnp.argsort(orders, axis=1, stable=True)
    packets = jnp.array([15, 15, 15, 15, 15, 15, 15, 3] + [0] * 8, dtype=jnp.int32)
    extras = jnp.take(packets, inverse)
    full_group = jax.random.randint(jax.random.fold_in(key, 12), (), 0, groups)
    heavy_owner = jax.random.randint(jax.random.fold_in(key, 13), (), 0, 4)
    slot_owner = jnp.arange(16, dtype=jnp.int32) // 4
    heavy_slot = slot_owner == heavy_owner
    other_slot = jnp.logical_not(heavy_slot)
    other_rank = jnp.cumsum(other_slot.astype(jnp.int32)) - 1
    rest_table = jnp.array([15, 15, 15, 3] + [0] * 12, dtype=jnp.int32)
    rest = jnp.take(rest_table, jnp.clip(other_rank, 0, 15))
    filled = jnp.where(heavy_slot, 15, jnp.where(other_slot, rest, 0)).astype(jnp.int32)
    chosen = (jnp.arange(groups, dtype=jnp.int32) == full_group)[:, None]
    extras = jnp.where(chosen, filled[None, :], extras)
    return (TILE * (1 + extras)).reshape(REGIONS).astype(jnp.int32)


def steps_of(key, extent, pieces, low, top_value):
    def one(axis_at, parts):
        draws = jax.random.uniform(jax.random.fold_in(jax.random.fold_in(key, 6), axis_at), (parts,), jnp.float32, low / len(pieces), top_value / len(pieces))
        return jnp.repeat(jnp.exp(draws), extent[axis_at] // parts).reshape((-1,) + (1,) * (len(extent) - axis_at - 1))

    factor_of = one(*pieces[0])
    for cut in pieces[1:]:
        factor_of = factor_of * one(*cut)
    return factor_of


def noise(own_key, dims, scale, most, cuts=(), kind=jnp.bfloat16):
    result = jax.random.normal(own_key, dims, jnp.float32) * scale
    if len(cuts) > 0:
        result = steps_of(own_key, dims, cuts, -0.22, 0.18) * result
    return jnp.clip(result, min=-most, max=most).astype(kind)


def setup_inputs(seed: int = 0) -> dict:
    splits = jax.random.split(jax.random.key(seed), 7)
    return {
        "tokens": noise(splits[0], (N_REGION * CAP, D), 1.0, 6.0, ((0, 32), (1, 16))),
        "cotangent": noise(splits[1], (N_REGION * CAP, D), 1.0, 6.0, ((0, 32), (1, 16))),
        "gain": jnp.clip(1.0 + 0.18 * jax.random.normal(splits[2], (D,), jnp.float32), 0.1, 1.9),
        "w_up": noise(splits[3], (D, FF), D ** -0.5, 0.1875, ((1, 16),)),
        "w_down": noise(splits[4], (FF, D), FF ** -0.5, 0.09375, ((0, 16),)),
        "counts": draw_counts(jax.random.fold_in(splits[6], 71), 0),
    }


EPSILON = 1e-05

def gelu_tanh(inputs):
    return jax.nn.gelu(inputs, approximate=True)

def reference(tokens, cotangent, gain, w_up, w_down, counts):
    all_loads = lax.optimization_barrier(jnp.sum(counts.reshape(N_REGION, REG_DEV), axis=1)).astype(jnp.int32)
    load_ends = jnp.cumsum(all_loads).astype(jnp.int32)
    load_starts = load_ends - all_loads
    places = jnp.arange(TOTAL, dtype=jnp.int32)
    owner_index = lax.optimization_barrier(jnp.sum((load_ends[None, :] <= places[:, None]).astype(jnp.int32), axis=1)).astype(jnp.int32)
    owner_start = jnp.take(load_starts, owner_index)
    flat_index = (owner_index * CAP + places - owner_start).astype(jnp.int32)
    rows_x = jnp.take(tokens, flat_index, axis=0).reshape(N_REGION, BAL, D)
    rows_dy = jnp.take(cotangent, flat_index, axis=0).reshape(N_REGION, BAL, D)
    group_width = FF // N_MP

    def layer_block(totals, block_item):
        block_x, block_dy = block_item
        whole_float = block_x.astype(jnp.float32)
        inv_rms = lax.rsqrt(lax.optimization_barrier(jnp.mean(whole_float * whole_float, axis=1)) + EPSILON)
        normed = (whole_float * inv_rms[:, None] * gain).astype(jnp.bfloat16)
        hidden = jnp.dot(normed, w_up, preferred_element_type=jnp.float32)
        activated, gelu_back = jax.vjp(gelu_tanh, hidden)
        act_rows = activated.astype(jnp.bfloat16)
        d_act = jnp.dot(block_dy, w_down.T, preferred_element_type=jnp.float32)
        d_hidden = gelu_back(d_act)[0].astype(jnp.bfloat16)
        grouped_h = d_hidden.astype(jnp.float32).reshape(BAL, N_MP, group_width)
        grouped_w = w_up.astype(jnp.float32).reshape(D, N_MP, group_width)
        partial_term = jnp.einsum('rmf,dmf->mrd', grouped_h, grouped_w)
        rounded = lax.optimization_barrier(partial_term.astype(jnp.bfloat16))
        d_normed = lax.optimization_barrier(jnp.sum(rounded.astype(jnp.float32), axis=0))
        weighted = gain * d_normed
        row_dot = lax.optimization_barrier(jnp.sum(weighted * whole_float, axis=1))
        cubed = inv_rms * inv_rms * inv_rms
        d_rows = block_dy.astype(jnp.float32) + weighted * inv_rms[:, None] - whole_float * (row_dot * cubed / D)[:, None]
        up_total, down_total, gain_total = totals
        up_total = up_total + jnp.dot(normed.T, d_hidden, preferred_element_type=jnp.float32)
        down_total = down_total + jnp.dot(act_rows.T, block_dy, preferred_element_type=jnp.float32)
        gain_total = gain_total + lax.optimization_barrier(jnp.sum(d_normed * whole_float * inv_rms[:, None], axis=0))
        return ((up_total, down_total, gain_total), d_rows.astype(jnp.bfloat16))
    start_totals = (jnp.zeros((D, FF), jnp.float32), jnp.zeros((FF, D), jnp.float32), jnp.zeros((D,), jnp.float32))
    totals, d_rows = lax.scan(layer_block, start_totals, (rows_x, rows_dy))
    grad_scale = 1.0 / math.sqrt(TOTAL)
    d_tokens = jnp.zeros((N_REGION * CAP, D), jnp.bfloat16).at[flat_index].set(d_rows.reshape(TOTAL, D))
    return (d_tokens, totals[0] * grad_scale, totals[1] * grad_scale, totals[2] * grad_scale)
```

```python
import functools
import math

import jax
import jax.numpy as jnp
from jax import lax
from jax.experimental import pallas as pl
from jax.experimental.pallas import tpu as pltpu
from jax.sharding import PartitionSpec as P

BAL = 496
EPSILON = 1e-05
MESH = pl.DeviceIdType.MESH
F32 = jnp.float32
BF16 = jnp.bfloat16
NCH = 4
GC = math.sqrt(2.0 / math.pi)


def nt_dot(a, b):
    return lax.dot_general(a, b, (((1,), (1,)), ((), ())), preferred_element_type=F32)


def nn_dot(a, b):
    return lax.dot_general(a, b, (((1,), (0,)), ((), ())), preferred_element_type=F32)


def kernel(
    X, Z, Y, s,
    x_hbm, d_hbm, gain_ref, wu_hbm, wd_hbm, counts_ref,
    dtok_ref, dup_ref, ddn_ref, dgain_ref,
    B, wu, wd, wg, wgT, gainb, Q, Qs, RSs, RSr, U, V, Gs, Xr, Ss, Zr,
    g1, g1r, g2, gy, g3, gx, g4, gz, live_s,
    loc, ag_s, ag_r, sb_s, sb_r, qs_s, qs_r, rs_s, rs_r, x_s, x_r, z_s, z_r,
    ga_s, ga_r, gy_s, gy_r, gx_s, gx_r, gz_s, gz_r,
):
    r = lax.axis_index("region")
    m = lax.axis_index("mp")
    x, z = r // Z, r % Z
    y, c = m // 2, m % 2
    H2 = Y // 2
    TC = B.shape[3]
    FB = B.shape[2] // 2
    D = wu.shape[0]
    FH = wu.shape[1]
    sib = (r, y * 2 + 1 - c)

    def ydev(k):
        return (r, ((y + k + Y) % Y) * 2 + c)

    def xdev(k):
        return (((x + k) % X) * Z + z, m)

    def zdev(k):
        return (x * Z + (z + k) % Z, m)

    bar = pltpu.get_barrier_semaphore()
    peers = [sib] + [ydev(k) for k in range(1, Y)] + [xdev(k) for k in range(1, X)]
    peers += [zdev(k) for k in range(1, Z)]
    for p in peers:
        pl.semaphore_signal(bar, 1, device_id=p, device_id_type=MESH)

    own = []
    for k in range(NCH):
        lanes = pl.ds(k * TC, TC)
        own.append(pltpu.make_async_copy(x_hbm.at[:, lanes], B.at[k, m, pl.ds(0, FB)], loc.at[2 * k]))
        own.append(pltpu.make_async_copy(d_hbm.at[:, lanes], B.at[k, m, pl.ds(FB, FB)], loc.at[2 * k + 1]))
    wcp = [
        pltpu.make_async_copy(wu_hbm, wu, loc.at[2 * NCH]),
        pltpu.make_async_copy(wd_hbm, wd, loc.at[2 * NCH + 1]),
    ]
    for cp in own + wcp:
        cp.start()
    load = counts_ref[0] + counts_ref[1] + counts_ref[2] + counts_ref[3]
    for k in range(NCH):
        at = lax.broadcasted_iota(jnp.int32, (1, TC), 1) + k * TC
        live_s[k] = jnp.where(at < load, 1.0, 0.0).astype(F32)
    for cp in own:
        cp.wait()
    pl.semaphore_wait(bar, len(peers))

    pending = []

    def remote(src, dst, ss, rs, dev):
        return pltpu.make_async_remote_copy(
            src_ref=src, dst_ref=dst, send_sem=ss, recv_sem=rs, device_id=dev, device_id_type=MESH
        )

    def go(cp):
        cp.start()
        pending.append(cp)

    def ag(d, h, k):
        sg = 1 if d == 0 else -1
        slot = ((y - sg * (h - 1) + Y) % Y) * 2 + c
        ref = B.at[k, slot] if h < H2 else B.at[k, slot, pl.ds(d * FB, FB)]
        return remote(ref, ref, ag_s.at[d, h - 1, k], ag_r.at[d, h - 1, k], ydev(sg))

    def sb(j, k):
        ref = B.at[k, ((y + j + Y) % Y) * 2 + c]
        return remote(ref, ref, sb_s.at[j % Y, k], sb_r.at[j % Y, k], sib)

    def own_send(k):
        go(ag(0, 1, k))
        go(ag(1, 1, k))
        go(sb(0, k))

    def arrive(h, k):
        for d in range(2):
            sg = 1 if d == 0 else -1
            ag(d, h, k).wait_recv()
            if h < H2:
                go(ag(d, h + 1, k))
                go(sb(-sg * h, k))
        if h == H2:
            go(sb(H2, k))

    def prep():
        gb = jnp.broadcast_to(gain_ref[...], (128, D)).T
        gainb[...] = gb.reshape(gainb.shape)
        wcp[0].wait()
        for j in range(FH // 128):
            t = wu[:, pl.ds(j * 128, 128)].astype(F32) * gb
            wg[:, pl.ds(j * 128, 128)] = t.astype(BF16)
            wgT[pl.ds(j * 128, 128), :] = t.T.astype(BF16)
        wcp[1].wait()

    def compute(k):
        for j in range(Y):
            sb(j, k).wait_recv()
        last = k == NCH - 1
        xc = B[k, :, 0:FB, :].reshape(D, TC)
        dc = B[k, :, FB : 2 * FB, :].reshape(D, TC)
        xf = xc.astype(F32)
        inv = lax.rsqrt(jnp.sum(xf * xf, axis=0, keepdims=True) * (1.0 / D) + EPSILON)
        live = live_s[k]
        v = nn_dot(wgT[...], xc) * inv
        a = nn_dot(wd[...], dc)
        v2 = v * v
        t = jnp.tanh(GC * v * (1.0 + 0.044715 * v2))
        cdf = 0.5 + 0.5 * t
        act = (v * cdf * live).astype(BF16)
        gp = cdf + (0.5 * GC) * v * (1.0 - t * t) * (1.0 + (3 * 0.044715) * v2)
        dh = a * gp * (live * inv)
        ct = jnp.sum(dh * v, axis=0, keepdims=True) * inv * (1.0 / D)
        dhb = dh.astype(BF16)

        def grads(u, lhs, rhs, acc):
            term = nt_dot(lhs, rhs)
            if k > 0:
                term = acc[...] + term
            acc[...] = term
            if last:
                Gs[u] = term.astype(BF16).reshape(Gs.shape[1:])
                for i in range(1, X):
                    go(xstage(u, i))

        grads(0, xc, dhb, U)
        if last:
            wuu = (wu[...].astype(F32) * U[...]).astype(BF16)
            gv = nt_dot(jnp.ones((8, FH), BF16), wuu)
            for j in range(Y):
                g1[j] = gv[:, j * 128 : (j + 1) * 128]
            go(gacopy())
        grads(1, dc, act, V)
        q = nn_dot(wg[...], dhb) - B[k, :, 0:FB, :].reshape(D, TC).astype(F32) * ct
        q = q.astype(BF16)
        for j in range(2 * Y):
            Q[k, j % 2, j // 2] = q[j * FB : (j + 1) * FB, :]
        go(qcopy(k))

    def qcopy(k):
        return remote(Q.at[k, 1 - c], Qs.at[k], qs_s.at[k], qs_r.at[k], sib)

    def gacopy():
        return remote(g1, g1r, ga_s, ga_r, sib)

    def xstage(u, i):
        return remote(
            Gs.at[u, (x + i) % X], Xr.at[u, i - 1], x_s.at[u, i - 1], x_r.at[u, i - 1], xdev(i)
        )

    def zstage(u, i):
        return remote(
            Ss.at[u, (z + i) % Z], Zr.at[u, i - 1], z_s.at[u, i - 1], z_r.at[u, i - 1], zdev(i)
        )

    def rs(d, h, k):
        sg = 1 if d == 0 else -1
        if h < H2:
            src, dst = RSs.at[d, h - 1, k], RSr.at[d, h - 1, k]
        else:
            src = RSs.at[d, h - 1, k, pl.ds(0, FB // 2)]
            dst = RSr.at[d, h - 1, k, pl.ds(0, FB // 2)]
        return remote(src, dst, rs_s.at[d, h - 1, k], rs_r.at[d, h - 1, k], ydev(sg))

    def came(d, h, k):
        rs(d, h, k).wait_recv()
        if h < H2:
            return RSr[d, h - 1, k].astype(F32)
        half = RSr[d, h - 1, k, 0 : FB // 2, :].astype(F32)
        zero = jnp.zeros_like(half)
        return jnp.concatenate([half, zero] if d == 0 else [zero, half], axis=0)

    def both(ty, k):
        return Q[k, c, ty].astype(F32) + Qs[k, ty].astype(F32)

    def rs_step(h, k):
        if h == H2:
            qcopy(k).wait_recv()
            p = both((y + H2) % Y, k).astype(BF16)
            RSs[0, h - 1, k, 0 : FB // 2, :] = p[0 : FB // 2, :]
            RSs[1, h - 1, k, 0 : FB // 2, :] = p[FB // 2 :, :]
            for d in range(2):
                go(rs(d, h, k))
            return
        for d in range(2):
            sg = 1 if d == 0 else -1
            p = both((y + sg * h + Y) % Y, k) + came(d, h + 1, k)
            RSs[d, h - 1, k] = p.astype(BF16)
            go(rs(d, h, k))

    def rs_end(k):
        tot = both(y, k) + came(0, 1, k) + came(1, 1, k)
        tot = B[k, m, FB : 2 * FB, :].astype(F32) + tot
        dtok_ref[:, pl.ds(k * TC, TC)] = (tot * live_s[k]).astype(BF16)

    def gain_a():
        gacopy().wait_recv()
        g2[...] = g1[...] + g1r[...]
        for i in range(1, Y):
            go(gycopy(i))

    def gycopy(i):
        return remote(g2.at[(y + i) % Y], gy.at[i - 1], gy_s.at[i - 1], gy_r.at[i - 1], ydev(i))

    def gxcopy(i):
        return remote(g3, gx.at[i - 1], gx_s.at[i - 1], gx_r.at[i - 1], xdev(i))

    def gzcopy(i):
        return remote(g4, gz.at[i - 1], gz_s.at[i - 1], gz_r.at[i - 1], zdev(i))

    def gain_x():
        t = g2[y]
        for i in range(1, Y):
            gycopy(i).wait_recv()
            t = t + gy[i - 1]
        g3[...] = t
        for i in range(1, X):
            go(gxcopy(i))

    def gain_z():
        t = g3[...]
        for i in range(1, X):
            gxcopy(i).wait_recv()
            t = t + gx[i - 1]
        g4[...] = t
        for i in range(1, Z):
            go(gzcopy(i))

    def gain_end():
        t = g4[...]
        for i in range(1, Z):
            gzcopy(i).wait_recv()
            t = t + gz[i - 1]
        t = t * s
        dgain_ref[...] = jnp.where(c == 0, t[0:1, 0:FB], t[0:1, FB : 2 * FB])

    def x_end(u):
        t = Gs[u, x].astype(F32)
        for i in range(1, X):
            xstage(u, i).wait_recv()
            t = t + Xr[u, i - 1].astype(F32)
        Ss[u] = t.astype(BF16)
        for i in range(1, Z):
            go(zstage(u, i))

    def z_end(u):
        t = Ss[u, z].astype(F32)
        for i in range(1, Z):
            zstage(u, i).wait_recv()
            t = t + Zr[u, i - 1].astype(F32)
        t = t * s
        if u == 0:
            gb = gainb[r]
            for j in range(FH // 128):
                dup_ref[:, pl.ds(j * 128, 128)] = t[:, j * 128 : (j + 1) * 128] * gb
        else:
            ddn_ref[...] = t

    own_send(0)
    own_send(1)
    prep()
    order = sorted(
        [(h + k, -h, h, k) for h in range(1, H2 + 1) for k in range(NCH)]
    )
    ready = []
    for at, (_, _, h, k) in enumerate(order):
        arrive(h, k)
        if h == 1 and k + 2 < NCH:
            own_send(k + 2)
        if ready:
            compute(ready.pop(0))
        if h == H2:
            ready.append(k)
    for k in ready:
        compute(k)

    steps = sorted([(H2 - h + k, h, k) for h in range(1, H2 + 1) for k in range(NCH)])
    extra = {2: [gain_a], 5: [gain_x], 8: [gain_z, lambda: x_end(0)], 12: [lambda: x_end(1)]}
    for at, (_, h, k) in enumerate(steps):
        rs_step(h, k)
        for f in extra.get(at, []):
            f()
    if len(steps) < 13:
        for at in sorted(extra):
            if at >= len(steps):
                for f in extra[at]:
                    f()
    for k in range(NCH):
        rs_end(k)
    gain_end()
    z_end(0)
    z_end(1)
    for cp in pending:
        cp.wait_send()


def solution(mesh):
    R, M = mesh.shape["region"], mesh.shape["mp"]
    X = max(k for k in (1, 2, 4) if k * k <= R)
    Z, Y = R // X, M // 2
    s = 1.0 / math.sqrt(BAL * R)

    def on_device(tokens, cotangent, gain, w_up, w_down, counts):
        T, FB = tokens.shape
        D, FH = w_up.shape
        TC = T // NCH
        RW = D // R
        H2 = Y // 2
        dma = pltpu.SemaphoreType.DMA
        scratch = [
            pltpu.VMEM((NCH, M, 2 * FB, TC), BF16),
            pltpu.VMEM((D, FH), BF16),
            pltpu.VMEM((FH, D), BF16),
            pltpu.VMEM((D, FH), BF16),
            pltpu.VMEM((FH, D), BF16),
            pltpu.VMEM((R, RW, 128), F32),
            pltpu.VMEM((NCH, 2, Y, FB, TC), BF16),
            pltpu.VMEM((NCH, Y, FB, TC), BF16),
            pltpu.VMEM((2, H2, NCH, FB, TC), BF16),
            pltpu.VMEM((2, H2, NCH, FB, TC), BF16),
            pltpu.VMEM((D, FH), F32),
            pltpu.VMEM((D, FH), F32),
            pltpu.VMEM((2, X, Z, RW, FH), BF16),
            pltpu.VMEM((2, X, Z, RW, FH), BF16),
            pltpu.VMEM((2, Z, RW, FH), BF16),
            pltpu.VMEM((2, Z, RW, FH), BF16),
            pltpu.VMEM((Y, 8, 128), F32),
            pltpu.VMEM((Y, 8, 128), F32),
            pltpu.VMEM((Y, 8, 128), F32),
            pltpu.VMEM((Y, 8, 128), F32),
            pltpu.VMEM((8, 128), F32),
            pltpu.VMEM((X, 8, 128), F32),
            pltpu.VMEM((8, 128), F32),
            pltpu.VMEM((Z, 8, 128), F32),
            pltpu.VMEM((NCH, 1, TC), F32),
            dma((2 * NCH + 2,)),
            dma((2, H2, NCH)),
            dma((2, H2, NCH)),
            dma((Y, NCH)),
            dma((Y, NCH)),
            dma((NCH,)),
            dma((NCH,)),
            dma((2, H2, NCH)),
            dma((2, H2, NCH)),
            dma((2, X)),
            dma((2, X)),
            dma((2, Z)),
            dma((2, Z)),
            dma,
            dma,
            dma((Y,)),
            dma((Y,)),
            dma((X,)),
            dma((X,)),
            dma((Z,)),
            dma((Z,)),
        ]
        hbm = pl.BlockSpec(memory_space=pl.ANY)
        vm = pl.BlockSpec(memory_space=pltpu.VMEM)
        sm = pl.BlockSpec(memory_space=pltpu.SMEM)
        dtok, dup, ddn, dgain = pl.pallas_call(
            functools.partial(kernel, X, Z, Y, s),
            out_shape=[
                jax.ShapeDtypeStruct((FB, T), BF16),
                jax.ShapeDtypeStruct((RW, FH), F32),
                jax.ShapeDtypeStruct((RW, FH), F32),
                jax.ShapeDtypeStruct((1, FB), F32),
            ],
            in_specs=[hbm, hbm, vm, hbm, hbm, sm],
            out_specs=[vm, vm, vm, vm],
            scratch_shapes=scratch,
            compiler_params=pltpu.CompilerParams(
                collective_id=0, has_side_effects=True, vmem_limit_bytes=44 << 20
            ),
            cost_estimate=pl.CostEstimate(
                flops=10 * T * D * FH, bytes_accessed=4 << 20, transcendentals=T * FH
            ),
        )(tokens.T, cotangent.T, gain.reshape(1, D), w_up, w_down, counts)
        return dtok.T, dup, ddn.T, dgain.reshape(FB)

    return jax.shard_map(
        on_device,
        mesh=mesh,
        in_specs=(
            P("region", "mp"), P("region", "mp"), P(), P(None, "mp"), P("mp", None), P("region"),
        ),
        out_specs=(P("region", "mp"), P("region", "mp"), P("mp", "region"), P("mp")),
        check_vma=False,
    )
```

```python
import functools
import math

import jax
import jax.numpy as jnp
from jax import lax
from jax.experimental import pallas as pl
from jax.experimental.pallas import tpu as pltpu
from jax.sharding import PartitionSpec as P

BAL = 496
EPSILON = 1e-05
MESH = pl.DeviceIdType.MESH
F32 = jnp.float32
BF16 = jnp.bfloat16
NCH = 4
ZFIRST = 1
HF = 128
GC = math.sqrt(2.0 / math.pi)


def nt_dot(a, b):
    return lax.dot_general(a, b, (((1,), (1,)), ((), ())), preferred_element_type=F32)


def nn_dot(a, b):
    return lax.dot_general(a, b, (((1,), (0,)), ((), ())), preferred_element_type=F32)


def order_of(H2):
    last = NCH - 1
    seq = [("own", 0, k) for k in range(NCH)] + [("prep", 0, 0)]
    seq += [("arrive", h, k) for h in range(1, H2) for k in range(NCH)]
    for k in range(NCH):
        seq.append(("arrive", H2, k))
        if 1 <= k < last:
            seq.append(("compute", 0, k - 1))
    far = [("rs", H2, k) for k in range(NCH)]
    near = [("rs", h, k) for h in range(H2 - 1, 0, -1) for k in range(NCH)]
    seq += [far[0], ("compute", 0, last - 1), far[1], ("compute", 0, last)] + far[2:]
    seq += near[:NCH] + [("gain_a", 0, 0)] + near[NCH : NCH + 2]
    seq += [("first", 0, 0), ("drain", 0, 0)] + near[NCH + 2 : 2 * NCH] + [("gain_x", 0, 0)]
    seq += [("first", 0, 1), ("first", 0, 2)] + near[2 * NCH :]
    seq += [("gain_z", 0, 0), ("rs_end", 0, 0), ("rs_end", 0, 1), ("first", 0, 3)]
    seq += [("rs_end", 0, k) for k in range(2, NCH)] + [("second", 0, 0), ("second", 0, 2)]
    return seq + [("gain_end", 0, 0), ("second", 0, 1), ("second", 0, 3)]


def kernel(
    X, Z, Y, s,
    x_hbm, d_hbm, gain_hbm, wu_hbm, wd_hbm, counts_hbm,
    dtok_ref, dup_ref, ddn_ref, dgain_ref,
    counts_ref, gain_ref, B, wu, wd, wg, wgT, gainb, Q, Qs, RSs, RSr, U, V, Gs, Xr, Ss, Zr, Gz, Zf, Sx, Xf,
    g1, g1r, g2, gy, g3, gx, g4, gz, live_s,
    loc, ag_s, ag_r, sb_s, sb_r, qs_s, qs_r, rs_s, rs_r, x_s, x_r, z_s, z_r,
    ga_s, ga_r, gy_s, gy_r, gx_s, gx_r, gz_s, gz_r,
):
    r = lax.axis_index("region")
    m = lax.axis_index("mp")
    x, z = r // Z, r % Z
    y, c = m // 2, m % 2
    H2 = Y // 2
    TC = B.shape[3]
    FB = B.shape[2] // 2
    D = wu.shape[0]
    FH = wu.shape[1]
    sib = (r, y * 2 + 1 - c)

    def ydev(k):
        return (r, ((y + k + Y) % Y) * 2 + c)

    def xdev(k):
        return (((x + k) % X) * Z + z, m)

    def zdev(k):
        return (x * Z + (z + k) % Z, m)

    bar = pltpu.get_barrier_semaphore()
    peers = [sib] + [ydev(k) for k in range(1, Y)] + [xdev(k) for k in range(1, X)]
    peers += [zdev(k) for k in range(1, Z)]
    for p in peers:
        pl.semaphore_signal(bar, 1, device_id=p, device_id_type=MESH)

    own = []
    for k in range(NCH):
        lanes = pl.ds(k * TC, TC)
        own.append(pltpu.make_async_copy(x_hbm.at[:, lanes], B.at[k, m, pl.ds(0, FB)], loc.at[2 * k]))
        own.append(pltpu.make_async_copy(d_hbm.at[:, lanes], B.at[k, m, pl.ds(FB, FB)], loc.at[2 * k + 1]))
    wcp = [
        pltpu.make_async_copy(wu_hbm, wu, loc.at[2 * NCH]),
        pltpu.make_async_copy(wd_hbm, wd, loc.at[2 * NCH + 1]),
        pltpu.make_async_copy(gain_hbm, gain_ref, loc.at[2 * NCH + 2]),
        pltpu.make_async_copy(counts_hbm, counts_ref, loc.at[2 * NCH + 3]),
    ]
    for cp in own + wcp:
        cp.start()
    wcp[3].wait()
    load = counts_ref[0] + counts_ref[1] + counts_ref[2] + counts_ref[3]
    for k in range(NCH):
        at = lax.broadcasted_iota(jnp.int32, (1, TC), 1) + k * TC
        live_s[k] = jnp.where(at < load, 1.0, 0.0).astype(F32)
    for cp in own:
        cp.wait()
    pl.semaphore_wait(bar, len(peers))

    pending = []

    def remote(src, dst, ss, rs, dev):
        return pltpu.make_async_remote_copy(
            src_ref=src, dst_ref=dst, send_sem=ss, recv_sem=rs, device_id=dev, device_id_type=MESH
        )

    def go(cp):
        cp.start()
        pending.append(cp)

    def ag(d, h, k):
        sg = 1 if d == 0 else -1
        slot = ((y - sg * (h - 1) + Y) % Y) * 2 + c
        ref = B.at[k, slot] if h < H2 else B.at[k, slot, pl.ds(d * FB, FB)]
        return remote(ref, ref, ag_s.at[d, h - 1, k], ag_r.at[d, h - 1, k], ydev(sg))

    def sb(j, k):
        ref = B.at[k, ((y + j + Y) % Y) * 2 + c]
        return remote(ref, ref, sb_s.at[j % Y, k], sb_r.at[j % Y, k], sib)

    def own_send(k):
        go(ag(0, 1, k))
        go(ag(1, 1, k))
        go(sb(0, k))

    def arrive(h, k):
        for d in range(2):
            sg = 1 if d == 0 else -1
            ag(d, h, k).wait_recv()
            if h < H2:
                go(ag(d, h + 1, k))
                go(sb(-sg * h, k))
        if h == H2:
            go(sb(H2, k))

    def prep():
        wcp[2].wait()
        gb = jnp.broadcast_to(gain_ref[...], (128, D)).T
        gainb[...] = gb.reshape(gainb.shape)
        wcp[0].wait()
        for j in range(FH // 128):
            t = wu[:, pl.ds(j * 128, 128)].astype(F32) * gb
            wg[:, pl.ds(j * 128, 128)] = t.astype(BF16)
            wgT[pl.ds(j * 128, 128), :] = t.T.astype(BF16)
        wcp[1].wait()

    def compute(k):
        for j in range(Y):
            sb(j, k).wait_recv()
        last = k == NCH - 1
        xc = B[k, :, 0:FB, :].reshape(D, TC)
        dc = B[k, :, FB : 2 * FB, :].reshape(D, TC)
        xf = xc.astype(F32)
        inv = lax.rsqrt(jnp.sum(xf * xf, axis=0, keepdims=True) * (1.0 / D) + EPSILON)
        live = live_s[k]
        v = nn_dot(wgT[...], xc) * inv
        a = nn_dot(wd[...], dc)
        v2 = v * v
        t = jnp.tanh(GC * v * (1.0 + 0.044715 * v2))
        cdf = 0.5 + 0.5 * t
        act = (v * cdf * live).astype(BF16)
        gp = cdf + (0.5 * GC) * v * (1.0 - t * t) * (1.0 + (3 * 0.044715) * v2)
        dh = a * gp * (live * inv)
        ct = jnp.sum(dh * v, axis=0, keepdims=True) * inv * (1.0 / D)
        dhb = dh.astype(BF16)

        def grads(u, lhs, rhs, acc):
            term = nt_dot(lhs, rhs)
            if k > 0:
                term = acc[...] + term
            acc[...] = term
            if last:
                for p in (2 * u + 1, 2 * u):
                    half = term[:, (p % 2) * HF : (p % 2) * HF + HF].astype(BF16)
                    half = half.reshape(X, Z, -1, HF)
                    if p == ZFIRST:
                        for i in range(X):
                            for j in range(Z):
                                Gz[j, i] = half[i, j]
                        for i in range(1, Z):
                            go(z_first(i))
                    else:
                        Gs[p] = half
                        for i in range(1, X):
                            go(xstage(p, i))

        grads(0, xc, dhb, U)
        if last:
            wuu = (wu[...].astype(F32) * U[...]).astype(BF16)
            gv = nt_dot(jnp.ones((8, FH), BF16), wuu)
            for j in range(Y):
                g1[j] = gv[:, j * 128 : (j + 1) * 128]
            go(gacopy())
        grads(1, dc, act, V)
        q = nn_dot(wg[...], dhb) - B[k, :, 0:FB, :].reshape(D, TC).astype(F32) * ct
        q = q.astype(BF16)
        for j in range(2 * Y):
            Q[k, j % 2, j // 2] = q[j * FB : (j + 1) * FB, :]
        go(qcopy(k))

    def qcopy(k):
        return remote(Q.at[k, 1 - c], Qs.at[k], qs_s.at[k], qs_r.at[k], sib)

    def gacopy():
        return remote(g1, g1r, ga_s, ga_r, sib)

    def xstage(p, i):
        return remote(
            Gs.at[p, (x + i) % X], Xr.at[p, i - 1], x_s.at[p, i - 1], x_r.at[p, i - 1], xdev(i)
        )

    def zstage(p, i):
        return remote(
            Ss.at[p, (z + i) % Z], Zr.at[p, i - 1], z_s.at[p, i - 1], z_r.at[p, i - 1], zdev(i)
        )

    def z_first(i):
        p = ZFIRST
        return remote(
            Gz.at[(z + i) % Z], Zf.at[i - 1], z_s.at[p, i - 1], z_r.at[p, i - 1], zdev(i)
        )

    def x_second(i):
        p = ZFIRST
        return remote(
            Sx.at[(x + i) % X], Xf.at[i - 1], x_s.at[p, i - 1], x_r.at[p, i - 1], xdev(i)
        )

    def rs(d, h, k):
        sg = 1 if d == 0 else -1
        if h < H2:
            src, dst = RSs.at[d, h - 1, k], RSr.at[d, h - 1, k]
        else:
            src = RSs.at[d, h - 1, k, pl.ds(0, FB // 2)]
            dst = RSr.at[d, h - 1, k, pl.ds(0, FB // 2)]
        return remote(src, dst, rs_s.at[d, h - 1, k], rs_r.at[d, h - 1, k], ydev(sg))

    def came(d, h, k):
        rs(d, h, k).wait_recv()
        if h < H2:
            return RSr[d, h - 1, k].astype(F32)
        half = RSr[d, h - 1, k, 0 : FB // 2, :].astype(F32)
        zero = jnp.zeros_like(half)
        return jnp.concatenate([half, zero] if d == 0 else [zero, half], axis=0)

    def both(ty, k):
        return Q[k, c, ty].astype(F32) + Qs[k, ty].astype(F32)

    def rs_step(h, k):
        if h == H2:
            qcopy(k).wait_recv()
            p = both((y + H2) % Y, k).astype(BF16)
            RSs[0, h - 1, k, 0 : FB // 2, :] = p[0 : FB // 2, :]
            RSs[1, h - 1, k, 0 : FB // 2, :] = p[FB // 2 :, :]
            for d in range(2):
                go(rs(d, h, k))
            return
        for d in range(2):
            sg = 1 if d == 0 else -1
            p = both((y + sg * h + Y) % Y, k) + came(d, h + 1, k)
            RSs[d, h - 1, k] = p.astype(BF16)
            go(rs(d, h, k))

    def rs_end(k):
        tot = both(y, k) + came(0, 1, k) + came(1, 1, k)
        tot = B[k, m, FB : 2 * FB, :].astype(F32) + tot
        dtok_ref[:, pl.ds(k * TC, TC)] = (tot * live_s[k]).astype(BF16)

    def gain_a():
        gacopy().wait_recv()
        g2[...] = g1[...] + g1r[...]
        for i in range(1, Y):
            go(gycopy(i))

    def gycopy(i):
        return remote(g2.at[(y + i) % Y], gy.at[i - 1], gy_s.at[i - 1], gy_r.at[i - 1], ydev(i))

    def gxcopy(i):
        return remote(g3, gx.at[i - 1], gx_s.at[i - 1], gx_r.at[i - 1], xdev(i))

    def gzcopy(i):
        return remote(g4, gz.at[i - 1], gz_s.at[i - 1], gz_r.at[i - 1], zdev(i))

    def gain_x():
        t = g2[y]
        for i in range(1, Y):
            gycopy(i).wait_recv()
            t = t + gy[i - 1]
        g3[...] = t
        for i in range(1, X):
            go(gxcopy(i))

    def gain_z():
        t = g3[...]
        for i in range(1, X):
            gxcopy(i).wait_recv()
            t = t + gx[i - 1]
        g4[...] = t
        for i in range(1, Z):
            go(gzcopy(i))

    def gain_end():
        t = g4[...]
        for i in range(1, Z):
            gzcopy(i).wait_recv()
            t = t + gz[i - 1]
        t = t * s
        dgain_ref[...] = jnp.where(c == 0, t[0:1, 0:FB], t[0:1, FB : 2 * FB])

    def first_end(p):
        if p == ZFIRST:
            t = Gz[z].astype(F32)
            for i in range(1, Z):
                z_first(i).wait_recv()
                t = t + Zf[i - 1].astype(F32)
            Sx[...] = t.astype(BF16)
            for i in range(1, X):
                go(x_second(i))
        else:
            t = Gs[p, x].astype(F32)
            for i in range(1, X):
                xstage(p, i).wait_recv()
                t = t + Xr[p, i - 1].astype(F32)
            Ss[p] = t.astype(BF16)
            for i in range(1, Z):
                go(zstage(p, i))

    def second_end(p):
        if p == ZFIRST:
            t = Sx[x].astype(F32)
            for i in range(1, X):
                x_second(i).wait_recv()
                t = t + Xf[i - 1].astype(F32)
        else:
            t = Ss[p, z].astype(F32)
            for i in range(1, Z):
                zstage(p, i).wait_recv()
                t = t + Zr[p, i - 1].astype(F32)
        t = t * s
        lanes = pl.ds((p % 2) * HF, HF)
        if p < 2:
            dup_ref[:, lanes] = t * gainb[r]
        else:
            ddn_ref[:, lanes] = t

    def drain():
        for cp in pending[:drained]:
            cp.wait_send()

    steps = {
        "own": lambda h, k: own_send(k),
        "prep": lambda h, k: prep(),
        "arrive": arrive,
        "compute": lambda h, k: compute(k),
        "rs": rs_step,
        "rs_end": lambda h, k: rs_end(k),
        "first": lambda h, k: first_end(k),
        "second": lambda h, k: second_end(k),
        "gain_a": lambda h, k: gain_a(),
        "gain_x": lambda h, k: gain_x(),
        "gain_z": lambda h, k: gain_z(),
        "gain_end": lambda h, k: gain_end(),
        "drain": lambda h, k: drain(),
    }
    for what, h, k in order_of(H2):
        if what == "compute":
            drained = len(pending) if k == 0 else drained
        steps[what](h, k)
    for cp in pending[drained:]:
        cp.wait_send()


def hand_out(*refs):
    n = (len(refs) - 2) // 3
    into, out = refs[-2], refs[-1]
    loads = [pltpu.make_async_copy(refs[i], refs[2 * n + i], into.at[i]) for i in range(n)]
    stores = [pltpu.make_async_copy(refs[2 * n + i], refs[n + i], out.at[i]) for i in range(n)]
    for cp in loads:
        cp.start()
    for cp, st in zip(loads, stores):
        cp.wait()
        st.start()
    for st in stores:
        st.wait()


def solution(mesh):
    R, M = mesh.shape["region"], mesh.shape["mp"]
    X = max(k for k in (1, 2, 4) if k * k <= R)
    Z, Y = R // X, M // 2
    s = 1.0 / math.sqrt(BAL * R)

    def on_device(tokens, cotangent, gain, w_up, w_down, counts):
        T, FB = tokens.shape
        D, FH = w_up.shape
        TC = T // NCH
        RW = D // R
        H2 = Y // 2
        dma = pltpu.SemaphoreType.DMA
        scratch = [
            pltpu.SMEM((4,), jnp.int32),
            pltpu.VMEM((1, D), F32),
            pltpu.VMEM((NCH, M, 2 * FB, TC), BF16),
            pltpu.VMEM((D, FH), BF16),
            pltpu.VMEM((FH, D), BF16),
            pltpu.VMEM((D, FH), BF16),
            pltpu.VMEM((FH, D), BF16),
            pltpu.VMEM((R, RW, 128), F32),
            pltpu.VMEM((NCH, 2, Y, FB, TC), BF16),
            pltpu.VMEM((NCH, Y, FB, TC), BF16),
            pltpu.VMEM((2, H2, NCH, FB, TC), BF16),
            pltpu.VMEM((2, H2, NCH, FB, TC), BF16),
            pltpu.VMEM((D, FH), F32),
            pltpu.VMEM((D, FH), F32),
            pltpu.VMEM((4, X, Z, RW, HF), BF16),
            pltpu.VMEM((4, X, Z, RW, HF), BF16),
            pltpu.VMEM((4, Z, RW, HF), BF16),
            pltpu.VMEM((4, Z, RW, HF), BF16),
            pltpu.VMEM((Z, X, RW, HF), BF16),
            pltpu.VMEM((Z, X, RW, HF), BF16),
            pltpu.VMEM((X, RW, HF), BF16),
            pltpu.VMEM((X, RW, HF), BF16),
            pltpu.VMEM((Y, 8, 128), F32),
            pltpu.VMEM((Y, 8, 128), F32),
            pltpu.VMEM((Y, 8, 128), F32),
            pltpu.VMEM((Y, 8, 128), F32),
            pltpu.VMEM((8, 128), F32),
            pltpu.VMEM((X, 8, 128), F32),
            pltpu.VMEM((8, 128), F32),
            pltpu.VMEM((Z, 8, 128), F32),
            pltpu.VMEM((NCH, 1, TC), F32),
            dma((2 * NCH + 4,)),
            dma((2, H2, NCH)),
            dma((2, H2, NCH)),
            dma((Y, NCH)),
            dma((Y, NCH)),
            dma((NCH,)),
            dma((NCH,)),
            dma((2, H2, NCH)),
            dma((2, H2, NCH)),
            dma((4, X)),
            dma((4, X)),
            dma((4, Z)),
            dma((4, Z)),
            dma,
            dma,
            dma((Y,)),
            dma((Y,)),
            dma((X,)),
            dma((X,)),
            dma((Z,)),
            dma((Z,)),
        ]
        hbm = pl.BlockSpec(memory_space=pltpu.HBM)
        vm = pl.BlockSpec(memory_space=pltpu.VMEM)
        shapes = [
            jax.ShapeDtypeStruct((FB, T), BF16),
            jax.ShapeDtypeStruct((RW, FH), F32),
            jax.ShapeDtypeStruct((RW, FH), F32),
            jax.ShapeDtypeStruct((1, FB), F32),
        ]
        sums = pl.pallas_call(
            functools.partial(kernel, X, Z, Y, s),
            out_shape=shapes,
            in_specs=[hbm] * 6,
            out_specs=[vm, vm, vm, vm],
            scratch_shapes=scratch,
            compiler_params=pltpu.CompilerParams(
                collective_id=0, has_side_effects=True, vmem_limit_bytes=56 << 20
            ),
            cost_estimate=pl.CostEstimate(
                flops=10 * T * D * FH, bytes_accessed=4 << 20, transcendentals=T * FH
            ),
        )(tokens.T, cotangent.T, gain.reshape(1, D), w_up, w_down, counts)
        dtok, dup, ddn, dgain = pl.pallas_call(
            hand_out,
            out_shape=shapes,
            in_specs=[hbm] * 4,
            out_specs=[hbm] * 4,
            scratch_shapes=[pltpu.VMEM(t.shape, t.dtype) for t in shapes] + [dma((4,)), dma((4,))],
            compiler_params=pltpu.CompilerParams(vmem_limit_bytes=56 << 20),
        )(*sums)
        return dtok.T, dup, ddn.T, dgain.reshape(FB)

    return jax.shard_map(
        on_device,
        mesh=mesh,
        in_specs=(
            P("region", "mp"), P("region", "mp"), P(), P(None, "mp"), P("mp", None), P("region"),
        ),
        out_specs=(P("region", "mp"), P("region", "mp"), P("mp", "region"), P("mp")),
        check_vma=False,
    )
```

```python
import functools
import math

import jax
import jax.numpy as jnp
from jax import lax
from jax.experimental import pallas as pl
from jax.experimental.pallas import tpu as pltpu
from jax.sharding import PartitionSpec as P

BAL = 496
EPSILON = 1e-05
MESH = pl.DeviceIdType.MESH
F32 = jnp.float32
BF16 = jnp.bfloat16
NCH = 4
ZFIRST = 1
HF = 128
GC = math.sqrt(2.0 / math.pi)


def nt_dot(a, b):
    return lax.dot_general(a, b, (((1,), (1,)), ((), ())), preferred_element_type=F32)


def nn_dot(a, b):
    return lax.dot_general(a, b, (((1,), (0,)), ((), ())), preferred_element_type=F32)


def order_of(H2):
    last = NCH - 1
    seq = [("own", 0, k) for k in range(NCH)] + [("prep", 0, 0)]
    for h in range(1, H2):
        seq += [("tell", h, 0)] + [("arrive", h, k) for k in range(NCH)]
    for k in range(NCH):
        seq.append(("arrive", H2, k))
        if 1 <= k < last:
            seq.append(("compute", 0, k - 1))
    far = [[("rs", H2, k), ("rs", H2 - 1, k)] for k in range(NCH)]
    near = [("rs", h, k) for h in range(H2 - 2, 0, -1) for k in range(NCH)]
    seq += far[0] + [("compute", 0, last - 1)] + far[1] + [("compute", 0, last)]
    seq += [near[0]] + far[2] + [near[1]] + far[3] + [("gain_a", 0, 0), ("drain", 0, 0)]
    seq += [near[2], ("first", 0, 0), near[4], near[3], near[5], ("gain_x", 0, 0)]
    seq += [near[6], ("first", 0, 3), ("first", 0, 1), near[7]]
    seq += [("rs_end", 0, 0), ("rs_end", 0, 1), ("gain_z", 0, 0), ("rs_end", 0, 2), ("first", 0, 2)]
    seq += [("rs_end", 0, 3), ("second", 0, 0), ("second", 0, 3)]
    return seq + [("gain_end", 0, 0), ("second", 0, 1), ("second", 0, 2)]


def kernel(
    X, Z, Y, s,
    x_hbm, d_hbm, gain_hbm, wu_hbm, wd_hbm, counts_hbm,
    dtok_ref, dup_ref, ddn_ref, dgain_ref,
    counts_ref, gain_ref, B, wu, wd, wg, wgT, gainb, Q, Qs, RSs, RSr, U, V, Gs, Xr, Ss, Zr, Gz, Zf, Sx, Xf,
    g1, g1r, g2, gy, g3, gx, g4, gz, live_s,
    loc, ag_s, ag_r, sb_s, sb_r, qs_s, qs_r, rs_s, rs_r, x_s, x_r, z_s, z_r,
    ga_s, ga_r, gy_s, gy_r, gx_s, gx_r, gz_s, gz_r, told,
):
    r = lax.axis_index("region")
    m = lax.axis_index("mp")
    x, z = r // Z, r % Z
    y, c = m // 2, m % 2
    H2 = Y // 2
    TC = B.shape[3]
    FB = B.shape[2] // 2
    D = wu.shape[0]
    FH = wu.shape[1]
    sib = (r, y * 2 + 1 - c)

    def ydev(k):
        return (r, ((y + k + Y) % Y) * 2 + c)

    def xdev(k):
        return (((x + k + X) % X) * Z + z, m)

    def zdev(k):
        return (x * Z + (z + k + Z) % Z, m)

    bar = pltpu.get_barrier_semaphore()
    sides = [(ydev(1), 1, H2), (ydev(-1), 0, H2), (zdev(1), 3, Z // 2), (zdev(-1), 2, Z // 2)]
    sides += [(xdev(1), 5, X // 2), (xdev(-1), 4, X // 2)]
    peers = [sib] + [p for p, _, _ in sides]
    for p in peers:
        pl.semaphore_signal(bar, 1, device_id=p, device_id_type=MESH)

    own = []
    for k in range(NCH):
        lanes = pl.ds(k * TC, TC)
        own.append(pltpu.make_async_copy(x_hbm.at[:, lanes], B.at[k, m, pl.ds(0, FB)], loc.at[2 * k]))
        own.append(pltpu.make_async_copy(d_hbm.at[:, lanes], B.at[k, m, pl.ds(FB, FB)], loc.at[2 * k + 1]))
    wcp = [
        pltpu.make_async_copy(wu_hbm, wu, loc.at[2 * NCH]),
        pltpu.make_async_copy(wd_hbm, wd, loc.at[2 * NCH + 1]),
        pltpu.make_async_copy(gain_hbm, gain_ref, loc.at[2 * NCH + 2]),
        pltpu.make_async_copy(counts_hbm, counts_ref, loc.at[2 * NCH + 3]),
    ]
    for cp in own + wcp:
        cp.start()
    wcp[3].wait()
    load = counts_ref[0] + counts_ref[1] + counts_ref[2] + counts_ref[3]
    for k in range(NCH):
        at = lax.broadcasted_iota(jnp.int32, (1, TC), 1) + k * TC
        live_s[k] = jnp.where(at < load, 1.0, 0.0).astype(F32)
    for cp in own:
        cp.wait()
    pl.semaphore_wait(bar, len(peers))

    pending = []

    def tell(n):
        at = [i for i in range(6) if sides[i][2] > n]
        for i in at:
            pl.semaphore_signal(told.at[sides[i][1]], 1, device_id=sides[i][0], device_id_type=MESH)
        for i in at:
            pl.semaphore_wait(told.at[i], 1)

    def remote(src, dst, ss, rs, dev):
        return pltpu.make_async_remote_copy(
            src_ref=src, dst_ref=dst, send_sem=ss, recv_sem=rs, device_id=dev, device_id_type=MESH
        )

    def go(cp):
        cp.start()
        pending.append(cp)

    def ag(d, h, k):
        sg = 1 if d == 0 else -1
        slot = ((y - sg * (h - 1) + Y) % Y) * 2 + c
        ref = B.at[k, slot] if h < H2 else B.at[k, slot, pl.ds(d * FB, FB)]
        return remote(ref, ref, ag_s.at[d, h - 1, k], ag_r.at[d, h - 1, k], ydev(sg))

    def sb(j, k):
        ref = B.at[k, ((y + j + Y) % Y) * 2 + c]
        return remote(ref, ref, sb_s.at[j % Y, k], sb_r.at[j % Y, k], sib)

    def own_send(k):
        go(ag(0, 1, k))
        go(ag(1, 1, k))
        go(sb(0, k))

    def arrive(h, k):
        for d in range(2):
            sg = 1 if d == 0 else -1
            ag(d, h, k).wait_recv()
            if h < H2:
                go(ag(d, h + 1, k))
                go(sb(-sg * h, k))
        if h == H2:
            go(sb(H2, k))

    def prep():
        wcp[2].wait()
        gb = jnp.broadcast_to(gain_ref[...], (128, D)).T
        gainb[...] = gb.reshape(gainb.shape)
        wcp[0].wait()
        for j in range(FH // 128):
            t = wu[:, pl.ds(j * 128, 128)].astype(F32) * gb
            wg[:, pl.ds(j * 128, 128)] = t.astype(BF16)
            wgT[pl.ds(j * 128, 128), :] = t.T.astype(BF16)
        wcp[1].wait()

    def compute(k):
        for j in range(Y):
            sb(j, k).wait_recv()
        last = k == NCH - 1
        xc = B[k, :, 0:FB, :].reshape(D, TC)
        dc = B[k, :, FB : 2 * FB, :].reshape(D, TC)
        xf = xc.astype(F32)
        inv = lax.rsqrt(jnp.sum(xf * xf, axis=0, keepdims=True) * (1.0 / D) + EPSILON)
        live = live_s[k]
        v = nn_dot(wgT[...], xc) * inv
        a = nn_dot(wd[...], dc)
        v2 = v * v
        t = jnp.tanh(GC * v * (1.0 + 0.044715 * v2))
        cdf = 0.5 + 0.5 * t
        act = (v * cdf * live).astype(BF16)
        gp = cdf + (0.5 * GC) * v * (1.0 - t * t) * (1.0 + (3 * 0.044715) * v2)
        dh = a * gp * (live * inv)
        ct = jnp.sum(dh * v, axis=0, keepdims=True) * inv * (1.0 / D)
        dhb = dh.astype(BF16)

        def grads(u, lhs, rhs, acc):
            term = nt_dot(lhs, rhs)
            if k > 0:
                term = acc[...] + term
            acc[...] = term
            if last:
                for p in (2 * u + 1, 2 * u):
                    half = term[:, (p % 2) * HF : (p % 2) * HF + HF].astype(BF16)
                    half = half.reshape(X, Z, -1, HF)
                    if p == ZFIRST:
                        for i in range(X):
                            for j in range(Z):
                                Gz[j, i] = half[i, j]
                        for i in range(1, Z):
                            go(z_first(i))
                    else:
                        Gs[p] = half
                        for i in range(1, X):
                            go(xstage(p, i))

        grads(0, xc, dhb, U)
        if last:
            wuu = (wu[...].astype(F32) * U[...]).astype(BF16)
            gv = nt_dot(jnp.ones((8, FH), BF16), wuu)
            for j in range(Y):
                g1[j] = gv[:, j * 128 : (j + 1) * 128]
            go(gacopy())
        grads(1, dc, act, V)
        q = nn_dot(wg[...], dhb) - B[k, :, 0:FB, :].reshape(D, TC).astype(F32) * ct
        q = q.astype(BF16)
        for j in range(2 * Y):
            Q[k, j % 2, j // 2] = q[j * FB : (j + 1) * FB, :]
        go(qcopy(k))

    def qcopy(k):
        return remote(Q.at[k, 1 - c], Qs.at[k], qs_s.at[k], qs_r.at[k], sib)

    def gacopy():
        return remote(g1, g1r, ga_s, ga_r, sib)

    def xstage(p, i):
        return remote(
            Gs.at[p, (x + i) % X], Xr.at[p, i - 1], x_s.at[p, i - 1], x_r.at[p, i - 1], xdev(i)
        )

    def zstage(p, i):
        return remote(
            Ss.at[p, (z + i) % Z], Zr.at[p, i - 1], z_s.at[p, i - 1], z_r.at[p, i - 1], zdev(i)
        )

    def z_first(i):
        p = ZFIRST
        return remote(
            Gz.at[(z + i) % Z], Zf.at[i - 1], z_s.at[p, i - 1], z_r.at[p, i - 1], zdev(i)
        )

    def x_second(i):
        p = ZFIRST
        return remote(
            Sx.at[(x + i) % X], Xf.at[i - 1], x_s.at[p, i - 1], x_r.at[p, i - 1], xdev(i)
        )

    def rs(d, h, k):
        sg = 1 if d == 0 else -1
        if h < H2:
            src, dst = RSs.at[d, h - 1, k], RSr.at[d, h - 1, k]
        else:
            sg = 2 * sg
            src = RSs.at[d, h - 1, k, pl.ds(0, FB // 2)]
            dst = RSr.at[d, h - 1, k, pl.ds(0, FB // 2)]
        return remote(src, dst, rs_s.at[d, h - 1, k], rs_r.at[d, h - 1, k], ydev(sg))

    def came(d, h, k):
        rs(d, h, k).wait_recv()
        if h < H2:
            return RSr[d, h - 1, k].astype(F32)
        half = RSr[d, h - 1, k, 0 : FB // 2, :].astype(F32)
        zero = jnp.zeros_like(half)
        return jnp.concatenate([half, zero] if d == 0 else [zero, half], axis=0)

    def both(ty, k):
        return Q[k, c, ty].astype(F32) + Qs[k, ty].astype(F32)

    def rs_step(h, k):
        if h == H2:
            qcopy(k).wait_recv()
            p = both((y + H2) % Y, k).astype(BF16)
            RSs[0, h - 1, k, 0 : FB // 2, :] = p[0 : FB // 2, :]
            RSs[1, h - 1, k, 0 : FB // 2, :] = p[FB // 2 :, :]
            for d in range(2):
                go(rs(d, h, k))
            return
        for d in range(2):
            sg = 1 if d == 0 else -1
            p = both((y + sg * h + Y) % Y, k)
            if h < H2 - 1:
                p = p + came(d, h + 1, k)
            if h == H2 - 2:
                p = p + came(d, H2, k)
            RSs[d, h - 1, k] = p.astype(BF16)
            go(rs(d, h, k))

    def rs_end(k):
        tot = both(y, k) + came(0, 1, k) + came(1, 1, k)
        tot = B[k, m, FB : 2 * FB, :].astype(F32) + tot
        dtok_ref[:, pl.ds(k * TC, TC)] = (tot * live_s[k]).astype(BF16)

    def gain_a():
        gacopy().wait_recv()
        g2[...] = g1[...] + g1r[...]
        for i in range(1, Y):
            go(gycopy(i))

    def gycopy(i):
        return remote(g2.at[(y + i) % Y], gy.at[i - 1], gy_s.at[i - 1], gy_r.at[i - 1], ydev(i))

    def gxcopy(i):
        return remote(g3, gx.at[i - 1], gx_s.at[i - 1], gx_r.at[i - 1], xdev(i))

    def gzcopy(i):
        return remote(g4, gz.at[i - 1], gz_s.at[i - 1], gz_r.at[i - 1], zdev(i))

    def gain_x():
        t = g2[y]
        for i in range(1, Y):
            gycopy(i).wait_recv()
            t = t + gy[i - 1]
        g3[...] = t
        for i in range(1, X):
            go(gxcopy(i))

    def gain_z():
        t = g3[...]
        for i in range(1, X):
            gxcopy(i).wait_recv()
            t = t + gx[i - 1]
        g4[...] = t
        for i in range(1, Z):
            go(gzcopy(i))

    def gain_end():
        t = g4[...]
        for i in range(1, Z):
            gzcopy(i).wait_recv()
            t = t + gz[i - 1]
        t = t * s
        dgain_ref[...] = jnp.where(c == 0, t[0:1, 0:FB], t[0:1, FB : 2 * FB])

    def first_end(p):
        if p == ZFIRST:
            t = Gz[z].astype(F32)
            for i in range(1, Z):
                z_first(i).wait_recv()
                t = t + Zf[i - 1].astype(F32)
            Sx[...] = t.astype(BF16)
            for i in range(1, X):
                go(x_second(i))
        else:
            t = Gs[p, x].astype(F32)
            for i in range(1, X):
                xstage(p, i).wait_recv()
                t = t + Xr[p, i - 1].astype(F32)
            Ss[p] = t.astype(BF16)
            for i in range(1, Z):
                go(zstage(p, i))

    def second_end(p):
        if p == ZFIRST:
            t = Sx[x].astype(F32)
            for i in range(1, X):
                x_second(i).wait_recv()
                t = t + Xf[i - 1].astype(F32)
        else:
            t = Ss[p, z].astype(F32)
            for i in range(1, Z):
                zstage(p, i).wait_recv()
                t = t + Zr[p, i - 1].astype(F32)
        t = t * s
        lanes = pl.ds((p % 2) * HF, HF)
        if p < 2:
            dup_ref[:, lanes] = t * gainb[r]
        else:
            ddn_ref[:, lanes] = t

    def drain():
        for cp in pending[:drained]:
            cp.wait_send()

    steps = {
        "own": lambda h, k: own_send(k),
        "prep": lambda h, k: prep(),
        "arrive": arrive,
        "compute": lambda h, k: compute(k),
        "rs": rs_step,
        "rs_end": lambda h, k: rs_end(k),
        "first": lambda h, k: first_end(k),
        "second": lambda h, k: second_end(k),
        "gain_a": lambda h, k: gain_a(),
        "gain_x": lambda h, k: gain_x(),
        "gain_z": lambda h, k: gain_z(),
        "gain_end": lambda h, k: gain_end(),
        "drain": lambda h, k: drain(),
        "tell": lambda h, k: tell(h),
    }
    for what, h, k in order_of(H2):
        if what == "compute":
            drained = len(pending) if k == 0 else drained
        steps[what](h, k)
    for cp in pending[drained:]:
        cp.wait_send()


def hand_out(*refs):
    n = (len(refs) - 2) // 3
    into, out = refs[-2], refs[-1]
    loads = [pltpu.make_async_copy(refs[i], refs[2 * n + i], into.at[i]) for i in range(n)]
    stores = [pltpu.make_async_copy(refs[2 * n + i], refs[n + i], out.at[i]) for i in range(n)]
    for cp in loads:
        cp.start()
    for cp, st in zip(loads, stores):
        cp.wait()
        st.start()
    for st in stores:
        st.wait()


def solution(mesh):
    R, M = mesh.shape["region"], mesh.shape["mp"]
    X = max(k for k in (1, 2, 4) if k * k <= R)
    Z, Y = R // X, M // 2
    s = 1.0 / math.sqrt(BAL * R)

    def on_device(tokens, cotangent, gain, w_up, w_down, counts):
        T, FB = tokens.shape
        D, FH = w_up.shape
        TC = T // NCH
        RW = D // R
        H2 = Y // 2
        dma = pltpu.SemaphoreType.DMA
        scratch = [
            pltpu.SMEM((4,), jnp.int32),
            pltpu.VMEM((1, D), F32),
            pltpu.VMEM((NCH, M, 2 * FB, TC), BF16),
            pltpu.VMEM((D, FH), BF16),
            pltpu.VMEM((FH, D), BF16),
            pltpu.VMEM((D, FH), BF16),
            pltpu.VMEM((FH, D), BF16),
            pltpu.VMEM((R, RW, 128), F32),
            pltpu.VMEM((NCH, 2, Y, FB, TC), BF16),
            pltpu.VMEM((NCH, Y, FB, TC), BF16),
            pltpu.VMEM((2, H2, NCH, FB, TC), BF16),
            pltpu.VMEM((2, H2, NCH, FB, TC), BF16),
            pltpu.VMEM((D, FH), F32),
            pltpu.VMEM((D, FH), F32),
            pltpu.VMEM((4, X, Z, RW, HF), BF16),
            pltpu.VMEM((4, X, Z, RW, HF), BF16),
            pltpu.VMEM((4, Z, RW, HF), BF16),
            pltpu.VMEM((4, Z, RW, HF), BF16),
            pltpu.VMEM((Z, X, RW, HF), BF16),
            pltpu.VMEM((Z, X, RW, HF), BF16),
            pltpu.VMEM((X, RW, HF), BF16),
            pltpu.VMEM((X, RW, HF), BF16),
            pltpu.VMEM((Y, 8, 128), F32),
            pltpu.VMEM((Y, 8, 128), F32),
            pltpu.VMEM((Y, 8, 128), F32),
            pltpu.VMEM((Y, 8, 128), F32),
            pltpu.VMEM((8, 128), F32),
            pltpu.VMEM((X, 8, 128), F32),
            pltpu.VMEM((8, 128), F32),
            pltpu.VMEM((Z, 8, 128), F32),
            pltpu.VMEM((NCH, 1, TC), F32),
            dma((2 * NCH + 4,)),
            dma((2, H2, NCH)),
            dma((2, H2, NCH)),
            dma((Y, NCH)),
            dma((Y, NCH)),
            dma((NCH,)),
            dma((NCH,)),
            dma((2, H2, NCH)),
            dma((2, H2, NCH)),
            dma((4, X)),
            dma((4, X)),
            dma((4, Z)),
            dma((4, Z)),
            dma,
            dma,
            dma((Y,)),
            dma((Y,)),
            dma((X,)),
            dma((X,)),
            dma((Z,)),
            dma((Z,)),
            pltpu.SemaphoreType.REGULAR((6,)),
        ]
        hbm = pl.BlockSpec(memory_space=pltpu.HBM)
        vm = pl.BlockSpec(memory_space=pltpu.VMEM)
        shapes = [
            jax.ShapeDtypeStruct((FB, T), BF16),
            jax.ShapeDtypeStruct((RW, FH), F32),
            jax.ShapeDtypeStruct((RW, FH), F32),
            jax.ShapeDtypeStruct((1, FB), F32),
        ]
        sums = pl.pallas_call(
            functools.partial(kernel, X, Z, Y, s),
            out_shape=shapes,
            in_specs=[hbm] * 6,
            out_specs=[vm, vm, vm, vm],
            scratch_shapes=scratch,
            compiler_params=pltpu.CompilerParams(
                collective_id=0, has_side_effects=True, vmem_limit_bytes=56 << 20
            ),
            cost_estimate=pl.CostEstimate(
                flops=10 * T * D * FH, bytes_accessed=4 << 20, transcendentals=T * FH
            ),
        )(tokens.T, cotangent.T, gain.reshape(1, D), w_up, w_down, counts)
        dtok, dup, ddn, dgain = pl.pallas_call(
            hand_out,
            out_shape=shapes,
            in_specs=[hbm] * 4,
            out_specs=[hbm] * 4,
            scratch_shapes=[pltpu.VMEM(t.shape, t.dtype) for t in shapes] + [dma((4,)), dma((4,))],
            compiler_params=pltpu.CompilerParams(vmem_limit_bytes=56 << 20),
        )(*sums)
        return dtok.T, dup, ddn.T, dgain.reshape(FB)

    return jax.shard_map(
        on_device,
        mesh=mesh,
        in_specs=(
            P("region", "mp"), P("region", "mp"), P(), P(None, "mp"), P("mp", None), P("region"),
        ),
        out_specs=(P("region", "mp"), P("region", "mp"), P("mp", "region"), P("mp")),
        check_vma=False,
    )
```

```python
import functools
import math

import jax
import jax.numpy as jnp
from jax import lax
from jax.experimental import pallas as pl
from jax.experimental.pallas import tpu as pltpu
from jax.sharding import PartitionSpec as P

BAL = 496
EPSILON = 1e-05
MESH = pl.DeviceIdType.MESH
F32 = jnp.float32
BF16 = jnp.bfloat16
NCH = 4
ZFIRST = (1,)
HF = 128
GC = math.sqrt(2.0 / math.pi)


def nt_dot(a, b):
    return lax.dot_general(a, b, (((1,), (1,)), ((), ())), preferred_element_type=F32)


def nn_dot(a, b):
    return lax.dot_general(a, b, (((1,), (0,)), ((), ())), preferred_element_type=F32)


def order_of(H2):
    last = NCH - 1
    seq = [("own", 0, k) for k in range(NCH)] + [("prep", 0, 0)]
    for h in range(1, H2):
        seq += [("tell", h - 1, 0)] if h > 1 else []
        seq += [("arrive", h, k) for k in range(NCH)]
    seq.append(("tell", H2 - 1, 0))
    for k in range(NCH):
        seq.append(("arrive", H2, k))
        if 1 <= k < last:
            seq.append(("compute", 0, k - 1))
    seq.append(("hear", H2 - 1, 0))
    far = [[("rs", H2, k), ("rs", H2 - 1, k)] for k in range(NCH)]
    near = [("rs", h, k) for h in range(H2 - 2, 0, -1) for k in range(NCH)]
    term = [("terms", 0, k) for k in range(NCH)]
    one = {p: ("first", 0, p) for p in range(4)}
    two = {p: ("second", 0, p) for p in range(4)}
    seq += [("compute", 0, last - 1), ("compute", 0, last), ("gain", 0, 0)]
    seq += [term[0], ("gain_a", 0, 0), term[1]] + far[0] + [term[2]] + far[1]
    seq += [one[0], ("calm", 0, 0), ("gain_x", 0, 0), term[3]] + far[2] + far[3]
    seq += [one[3], near[0], one[1], near[1], ("gain_z", 0, 0), near[2], one[2], near[3]]
    seq += near[4:] + [("rs_end", 0, k) for k in range(NCH)]
    seq += [two[0], two[3], ("gain_end", 0, 0), ("drain", 0, 0), two[1], two[2]]
    return seq


def kernel(
    X, Z, Y, s,
    x_hbm, d_hbm, gain_hbm, wu_hbm, wd_hbm, counts_hbm,
    dtok_out, dup_out, ddn_out, dgain_out,
    dtok_ref, dup_ref, ddn_ref, dgain_ref,
    counts_ref, gain_ref, B, wu, wd, wg, wgT, gainb, Q, Qs, RSs, RSr, U, V, Gs, Xr, Ss, Zr, Gz, Zf, Sx, Xf,
    DH, CT, g1, g1r, g2, gy, g3, gx, g4, gz, live_s,
    loc, out_s, ag_s, ag_r, sb_s, sb_r, qs_s, qs_r, rs_s, rs_r, x_s, x_r, z_s, z_r,
    ga_s, ga_r, gy_s, gy_r, gx_s, gx_r, gz_s, gz_r, told,
):
    r = lax.axis_index("region")
    m = lax.axis_index("mp")
    x, z = r // Z, r % Z
    y, c = m // 2, m % 2
    H2 = Y // 2
    TC = B.shape[3]
    FB = B.shape[2] // 2
    D = wu.shape[0]
    FH = wu.shape[1]
    sib = (r, y * 2 + 1 - c)

    def ydev(k):
        return (r, ((y + k + Y) % Y) * 2 + c)

    def xdev(k):
        return (((x + k + X) % X) * Z + z, m)

    def zdev(k):
        return (x * Z + (z + k + Z) % Z, m)

    bar = pltpu.get_barrier_semaphore()
    sides = [(ydev(1), 1, H2), (ydev(-1), 0, H2), (zdev(1), 3, Z // 2), (zdev(-1), 2, Z // 2)]
    sides += [(xdev(1), 5, X // 2), (xdev(-1), 4, X // 2)]

    def greet(p):
        pl.semaphore_signal(bar, 1, device_id=p, device_id_type=MESH)

    for p in [sib, ydev(1), ydev(-1), xdev(1), xdev(-1)]:
        greet(p)
    pl.when(z < Z - 1)(lambda: greet(zdev(1)))
    pl.when(z > 0)(lambda: greet(zdev(-1)))

    own = []
    for k in range(NCH):
        lanes = pl.ds(k * TC, TC)
        own.append(pltpu.make_async_copy(x_hbm.at[:, lanes], B.at[k, m, pl.ds(0, FB)], loc.at[2 * k]))
        own.append(pltpu.make_async_copy(d_hbm.at[:, lanes], B.at[k, m, pl.ds(FB, FB)], loc.at[2 * k + 1]))
    wcp = [
        pltpu.make_async_copy(wu_hbm, wu, loc.at[2 * NCH]),
        pltpu.make_async_copy(wd_hbm, wd, loc.at[2 * NCH + 1]),
        pltpu.make_async_copy(gain_hbm, gain_ref, loc.at[2 * NCH + 2]),
        pltpu.make_async_copy(counts_hbm, counts_ref, loc.at[2 * NCH + 3]),
    ]
    for cp in own + wcp:
        cp.start()
    wcp[3].wait()
    load = counts_ref[0] + counts_ref[1] + counts_ref[2] + counts_ref[3]
    for k in range(NCH):
        at = lax.broadcasted_iota(jnp.int32, (1, TC), 1) + k * TC
        live_s[k] = jnp.where(at < load, 1.0, 0.0).astype(F32)
    for cp in own:
        cp.wait()
    pl.when(z == 0)(lambda: pl.semaphore_wait(bar, 6))
    pl.when(z > 0)(lambda: pl.semaphore_wait(bar, 7))
    pl.when(z == 0)(lambda: greet(zdev(-1)))
    pl.when(z == Z - 1)(lambda: greet(zdev(1)))

    pending = []

    def hear(n):
        for i in range(6):
            if sides[i][2] > n > 0:
                pl.semaphore_wait(told.at[i], 1)

    def tell(n):
        if n == 1:
            pl.when(z == 0)(lambda: pl.semaphore_wait(bar, 1))
        hear(n - 1)
        for peer, i, far in sides:
            if far > n:
                pl.semaphore_signal(told.at[i], 1, device_id=peer, device_id_type=MESH)

    given = []

    def give(src, dst):
        cp = pltpu.make_async_copy(src, dst, out_s.at[len(given)])
        cp.start()
        given.append(cp)

    def remote(src, dst, ss, rs, dev):
        return pltpu.make_async_remote_copy(
            src_ref=src, dst_ref=dst, send_sem=ss, recv_sem=rs, device_id=dev, device_id_type=MESH
        )

    def go(cp):
        cp.start()
        pending.append(cp)

    def ag(d, h, k):
        sg = 1 if d == 0 else -1
        slot = ((y - sg * (h - 1) + Y) % Y) * 2 + c
        ref = B.at[k, slot] if h < H2 else B.at[k, slot, pl.ds(d * FB, FB)]
        return remote(ref, ref, ag_s.at[d, h - 1, k], ag_r.at[d, h - 1, k], ydev(sg))

    def sb(j, k):
        ref = B.at[k, ((y + j + Y) % Y) * 2 + c]
        return remote(ref, ref, sb_s.at[j % Y, k], sb_r.at[j % Y, k], sib)

    def own_send(k):
        go(ag(0, 1, k))
        go(ag(1, 1, k))
        go(sb(0, k))

    def arrive(h, k):
        for d in range(2):
            sg = 1 if d == 0 else -1
            ag(d, h, k).wait_recv()
            if h < H2:
                go(ag(d, h + 1, k))
                go(sb(-sg * h, k))
        if h == H2:
            go(sb(H2, k))

    def prep():
        wcp[2].wait()
        gb = jnp.broadcast_to(gain_ref[...], (128, D)).T
        gainb[...] = gb.reshape(gainb.shape)
        wcp[0].wait()
        for j in range(FH // 128):
            t = wu[:, pl.ds(j * 128, 128)].astype(F32) * gb
            wg[:, pl.ds(j * 128, 128)] = t.astype(BF16)
            wgT[pl.ds(j * 128, 128), :] = t.T.astype(BF16)
        wcp[1].wait()

    def compute(k):
        for j in range(Y):
            sb(j, k).wait_recv()
        last = k == NCH - 1
        xc = B[k, :, 0:FB, :].reshape(D, TC)
        dc = B[k, :, FB : 2 * FB, :].reshape(D, TC)
        xf = xc.astype(F32)
        inv = lax.rsqrt(jnp.sum(xf * xf, axis=0, keepdims=True) * (1.0 / D) + EPSILON)
        live = live_s[k]
        v = nn_dot(wgT[...], xc) * inv
        a = nn_dot(wd[...], dc)
        v2 = v * v
        t = jnp.tanh(GC * v * (1.0 + 0.044715 * v2))
        cdf = 0.5 + 0.5 * t
        act = (v * cdf * live).astype(BF16)
        gp = cdf + (0.5 * GC) * v * (1.0 - t * t) * (1.0 + (3 * 0.044715) * v2)
        dh = a * gp * (live * inv)
        ct = jnp.sum(dh * v, axis=0, keepdims=True) * inv * (1.0 / D)
        dhb = dh.astype(BF16)

        def grads(u, lhs, rhs, acc):
            term = nt_dot(lhs, rhs)
            if k > 0:
                term = acc[...] + term
            acc[...] = term
            if last:
                for p in (2 * u + 1, 2 * u):
                    half = term[:, (p % 2) * HF : (p % 2) * HF + HF].astype(BF16)
                    half = half.reshape(X, Z, -1, HF)
                    if p in ZFIRST:
                        for i in range(X):
                            for j in range(Z):
                                Gz[p, j, i] = half[i, j]
                        for i in range(1, Z):
                            go(z_first(p, i))
                    else:
                        Gs[p] = half
                        for i in range(1, X):
                            go(xstage(p, i))

        grads(0, xc, dhb, U)
        grads(1, dc, act, V)
        DH[k] = dhb
        CT[k] = ct

    def gain_start():
        wuu = (wu[...].astype(F32) * U[...]).astype(BF16)
        gv = nt_dot(jnp.ones((8, FH), BF16), wuu)
        for j in range(Y):
            g1[j] = gv[:, j * 128 : (j + 1) * 128]
        go(gacopy())

    def terms(k):
        q = nn_dot(wg[...], DH[k]) - B[k, :, 0:FB, :].reshape(D, TC).astype(F32) * CT[k]
        q = q.astype(BF16)
        for j in range(2 * Y):
            Q[k, j % 2, j // 2] = q[j * FB : (j + 1) * FB, :]
        go(qcopy(k))

    def qcopy(k):
        return remote(Q.at[k, 1 - c], Qs.at[k], qs_s.at[k], qs_r.at[k], sib)

    def gacopy():
        return remote(g1, g1r, ga_s, ga_r, sib)

    def xstage(p, i):
        return remote(
            Gs.at[p, (x + i) % X], Xr.at[p, i - 1], x_s.at[p, i - 1], x_r.at[p, i - 1], xdev(i)
        )

    def zstage(p, i):
        return remote(
            Ss.at[p, (z + i) % Z], Zr.at[p, i - 1], z_s.at[p, i - 1], z_r.at[p, i - 1], zdev(i)
        )

    def z_first(p, i):
        return remote(
            Gz.at[p, (z + i) % Z], Zf.at[p, i - 1], z_s.at[p, i - 1], z_r.at[p, i - 1], zdev(i)
        )

    def x_second(p, i):
        return remote(
            Sx.at[p, (x + i) % X], Xf.at[p, i - 1], x_s.at[p, i - 1], x_r.at[p, i - 1], xdev(i)
        )

    def rs(d, h, k):
        sg = 1 if d == 0 else -1
        if h < H2:
            src, dst = RSs.at[d, h - 1, k], RSr.at[d, h - 1, k]
        else:
            sg = 2 * sg
            src = RSs.at[d, h - 1, k, pl.ds(0, FB // 2)]
            dst = RSr.at[d, h - 1, k, pl.ds(0, FB // 2)]
        return remote(src, dst, rs_s.at[d, h - 1, k], rs_r.at[d, h - 1, k], ydev(sg))

    def came(d, h, k):
        rs(d, h, k).wait_recv()
        if h < H2:
            return RSr[d, h - 1, k].astype(F32)
        half = RSr[d, h - 1, k, 0 : FB // 2, :].astype(F32)
        zero = jnp.zeros_like(half)
        return jnp.concatenate([half, zero] if d == 0 else [zero, half], axis=0)

    def both(ty, k):
        return Q[k, c, ty].astype(F32) + Qs[k, ty].astype(F32)

    def rs_step(h, k):
        if h == H2:
            qcopy(k).wait_recv()
            p = both((y + H2) % Y, k).astype(BF16)
            RSs[0, h - 1, k, 0 : FB // 2, :] = p[0 : FB // 2, :]
            RSs[1, h - 1, k, 0 : FB // 2, :] = p[FB // 2 :, :]
            for d in range(2):
                go(rs(d, h, k))
            return
        for d in range(2):
            sg = 1 if d == 0 else -1
            p = both((y + sg * h + Y) % Y, k)
            if h < H2 - 1:
                p = p + came(d, h + 1, k)
            if h == H2 - 2:
                p = p + came(d, H2, k)
            RSs[d, h - 1, k] = p.astype(BF16)
            go(rs(d, h, k))

    def rs_end(k):
        tot = both(y, k) + came(0, 1, k) + came(1, 1, k)
        tot = B[k, m, FB : 2 * FB, :].astype(F32) + tot
        lanes = pl.ds(k * TC, TC)
        dtok_ref[:, lanes] = (tot * live_s[k]).astype(BF16)
        give(dtok_ref.at[:, lanes], dtok_out.at[:, lanes])

    def gain_a():
        gacopy().wait_recv()
        g2[...] = g1[...] + g1r[...]
        for i in range(1, Y):
            go(gycopy(i))

    def gycopy(i):
        return remote(g2.at[(y + i) % Y], gy.at[i - 1], gy_s.at[i - 1], gy_r.at[i - 1], ydev(i))

    def gxcopy(i):
        return remote(g3, gx.at[i - 1], gx_s.at[i - 1], gx_r.at[i - 1], xdev(i))

    def gzcopy(i):
        return remote(g4, gz.at[i - 1], gz_s.at[i - 1], gz_r.at[i - 1], zdev(i))

    def gain_x():
        t = g2[y]
        for i in range(1, Y):
            gycopy(i).wait_recv()
            t = t + gy[i - 1]
        g3[...] = t
        for i in range(1, X):
            go(gxcopy(i))

    def gain_z():
        t = g3[...]
        for i in range(1, X):
            gxcopy(i).wait_recv()
            t = t + gx[i - 1]
        g4[...] = t
        for i in range(1, Z):
            go(gzcopy(i))

    def gain_end():
        t = g4[...]
        for i in range(1, Z):
            gzcopy(i).wait_recv()
            t = t + gz[i - 1]
        t = t * s
        dgain_ref[...] = jnp.where(c == 0, t[0:1, 0:FB], t[0:1, FB : 2 * FB])
        give(dgain_ref, dgain_out)

    def first_end(p):
        if p in ZFIRST:
            t = Gz[p, z].astype(F32)
            for i in range(1, Z):
                z_first(p, i).wait_recv()
                t = t + Zf[p, i - 1].astype(F32)
            Sx[p] = t.astype(BF16)
            for i in range(1, X):
                go(x_second(p, i))
        else:
            t = Gs[p, x].astype(F32)
            for i in range(1, X):
                xstage(p, i).wait_recv()
                t = t + Xr[p, i - 1].astype(F32)
            Ss[p] = t.astype(BF16)
            for i in range(1, Z):
                go(zstage(p, i))

    def second_end(p):
        if p in ZFIRST:
            t = Sx[p, x].astype(F32)
            for i in range(1, X):
                x_second(p, i).wait_recv()
                t = t + Xf[p, i - 1].astype(F32)
        else:
            t = Ss[p, z].astype(F32)
            for i in range(1, Z):
                zstage(p, i).wait_recv()
                t = t + Zr[p, i - 1].astype(F32)
        t = t * s
        lanes = pl.ds((p % 2) * HF, HF)
        if p < 2:
            dup_ref[:, lanes] = t * gainb[r]
            give(dup_ref.at[:, lanes], dup_out.at[:, lanes])
        else:
            ddn_ref[:, lanes] = t
            give(ddn_ref.at[:, lanes], ddn_out.at[:, lanes])

    def calm():
        for _ in range(NCH * (4 * H2 - 1)):
            pending.pop(0).wait_send()

    def drain():
        while pending:
            pending.pop().wait_send()

    steps = {
        "own": lambda h, k: own_send(k),
        "prep": lambda h, k: prep(),
        "arrive": arrive,
        "compute": lambda h, k: compute(k),
        "terms": lambda h, k: terms(k),
        "gain": lambda h, k: gain_start(),
        "rs": rs_step,
        "rs_end": lambda h, k: rs_end(k),
        "first": lambda h, k: first_end(k),
        "second": lambda h, k: second_end(k),
        "gain_a": lambda h, k: gain_a(),
        "gain_x": lambda h, k: gain_x(),
        "gain_z": lambda h, k: gain_z(),
        "gain_end": lambda h, k: gain_end(),
        "drain": lambda h, k: drain(),
        "calm": lambda h, k: calm(),
        "tell": lambda h, k: tell(h),
        "hear": lambda h, k: hear(h),
    }
    for what, h, k in order_of(H2):
        steps[what](h, k)
    drain()
    for cp in given:
        cp.wait()


def hand_out(*refs):
    n = (len(refs) - 2) // 3
    into, out = refs[-2], refs[-1]
    loads = [pltpu.make_async_copy(refs[i], refs[2 * n + i], into.at[i]) for i in range(n)]
    stores = [pltpu.make_async_copy(refs[2 * n + i], refs[n + i], out.at[i]) for i in range(n)]
    for cp in loads:
        cp.start()
    for cp, st in zip(loads, stores):
        cp.wait()
        st.start()
    for st in stores:
        st.wait()


def solution(mesh):
    R, M = mesh.shape["region"], mesh.shape["mp"]
    X = max(k for k in (1, 2, 4) if k * k <= R)
    Z, Y = R // X, M // 2
    s = 1.0 / math.sqrt(BAL * R)

    def on_device(tokens, cotangent, gain, w_up, w_down, counts):
        T, FB = tokens.shape
        D, FH = w_up.shape
        TC = T // NCH
        RW = D // R
        H2 = Y // 2
        dma = pltpu.SemaphoreType.DMA
        shapes = [
            jax.ShapeDtypeStruct((FB, T), BF16),
            jax.ShapeDtypeStruct((RW, FH), F32),
            jax.ShapeDtypeStruct((RW, FH), F32),
            jax.ShapeDtypeStruct((1, FB), F32),
        ]
        scratch = [pltpu.VMEM(t.shape, t.dtype) for t in shapes] + [
            pltpu.SMEM((4,), jnp.int32),
            pltpu.VMEM((1, D), F32),
            pltpu.VMEM((NCH, M, 2 * FB, TC), BF16),
            pltpu.VMEM((D, FH), BF16),
            pltpu.VMEM((FH, D), BF16),
            pltpu.VMEM((D, FH), BF16),
            pltpu.VMEM((FH, D), BF16),
            pltpu.VMEM((R, RW, 128), F32),
            pltpu.VMEM((NCH, 2, Y, FB, TC), BF16),
            pltpu.VMEM((NCH, Y, FB, TC), BF16),
            pltpu.VMEM((2, H2, NCH, FB, TC), BF16),
            pltpu.VMEM((2, H2, NCH, FB, TC), BF16),
            pltpu.VMEM((D, FH), F32),
            pltpu.VMEM((D, FH), F32),
            pltpu.VMEM((4, X, Z, RW, HF), BF16),
            pltpu.VMEM((4, X, Z, RW, HF), BF16),
            pltpu.VMEM((4, Z, RW, HF), BF16),
            pltpu.VMEM((4, Z, RW, HF), BF16),
            pltpu.VMEM((4, Z, X, RW, HF), BF16),
            pltpu.VMEM((4, Z, X, RW, HF), BF16),
            pltpu.VMEM((4, X, RW, HF), BF16),
            pltpu.VMEM((4, X, RW, HF), BF16),
            pltpu.VMEM((NCH, FH, TC), BF16),
            pltpu.VMEM((NCH, 1, TC), F32),
            pltpu.VMEM((Y, 8, 128), F32),
            pltpu.VMEM((Y, 8, 128), F32),
            pltpu.VMEM((Y, 8, 128), F32),
            pltpu.VMEM((Y, 8, 128), F32),
            pltpu.VMEM((8, 128), F32),
            pltpu.VMEM((X, 8, 128), F32),
            pltpu.VMEM((8, 128), F32),
            pltpu.VMEM((Z, 8, 128), F32),
            pltpu.VMEM((NCH, 1, TC), F32),
            dma((2 * NCH + 4,)),
            dma((NCH + 5,)),
            dma((2, H2, NCH)),
            dma((2, H2, NCH)),
            dma((Y, NCH)),
            dma((Y, NCH)),
            dma((NCH,)),
            dma((NCH,)),
            dma((2, H2, NCH)),
            dma((2, H2, NCH)),
            dma((4, X)),
            dma((4, X)),
            dma((4, Z)),
            dma((4, Z)),
            dma,
            dma,
            dma((Y,)),
            dma((Y,)),
            dma((X,)),
            dma((X,)),
            dma((Z,)),
            dma((Z,)),
            pltpu.SemaphoreType.REGULAR((6,)),
        ]
        hbm = pl.BlockSpec(memory_space=pltpu.HBM)
        sums = pl.pallas_call(
            functools.partial(kernel, X, Z, Y, s),
            out_shape=shapes,
            in_specs=[hbm] * 6,
            out_specs=[hbm] * 4,
            scratch_shapes=scratch,
            compiler_params=pltpu.CompilerParams(
                collective_id=0, has_side_effects=True, vmem_limit_bytes=56 << 20
            ),
            cost_estimate=pl.CostEstimate(
                flops=10 * T * D * FH, bytes_accessed=4 << 20, transcendentals=T * FH
            ),
        )(tokens.T, cotangent.T, gain.reshape(1, D), w_up, w_down, counts)
        dtok, dup, ddn, dgain = pl.pallas_call(
            hand_out,
            out_shape=shapes,
            in_specs=[hbm] * 4,
            out_specs=[hbm] * 4,
            scratch_shapes=[pltpu.VMEM(t.shape, t.dtype) for t in shapes] + [dma((4,)), dma((4,))],
            compiler_params=pltpu.CompilerParams(vmem_limit_bytes=56 << 20),
        )(*sums)
        return dtok.T, dup, ddn.T, dgain.reshape(FB)

    return jax.shard_map(
        on_device,
        mesh=mesh,
        in_specs=(
            P("region", "mp"), P("region", "mp"), P(), P(None, "mp"), P("mp", None), P("region"),
        ),
        out_specs=(P("region", "mp"), P("region", "mp"), P("mp", "region"), P("mp")),
        check_vma=False,
    )
```

```python
import functools
import math

import jax
import jax.numpy as jnp
from jax import lax
from jax.experimental import pallas as pl
from jax.experimental.pallas import tpu as pltpu
from jax.sharding import PartitionSpec as P

BAL = 496
EPSILON = 1e-05
MESH = pl.DeviceIdType.MESH
F32 = jnp.float32
BF16 = jnp.bfloat16
NCH = 4
ZFIRST = (1,)
HF = 128
GC = math.sqrt(2.0 / math.pi)


def nt_dot(a, b):
    return lax.dot_general(a, b, (((1,), (1,)), ((), ())), preferred_element_type=F32)


def nn_dot(a, b):
    return lax.dot_general(a, b, (((1,), (0,)), ((), ())), preferred_element_type=F32)


def order_of(H2):
    last = NCH - 1
    seq = [("own", 0, k) for k in range(NCH)] + [("prep", 0, 0)]
    for h in range(1, H2):
        seq += [("tell", h - 1, 0)] if h > 1 else []
        seq += [("arrive", h, k) for k in range(NCH)]
    seq.append(("tell", H2 - 1, 0))
    for k in range(NCH):
        seq.append(("arrive", H2, k))
        if 1 <= k < last:
            seq.append(("compute", 0, k - 1))
    seq += [("hear", H2 - 1, 0), ("upper", 0, 0)]
    far = [[("rs", H2, k), ("rs", H2 - 1, k)] for k in range(NCH)]
    near = [("rs", h, k) for h in range(H2 - 2, 0, -1) for k in range(NCH)]
    term = [("terms", 0, k) for k in range(NCH)]
    one = {p: ("first", 0, p) for p in range(4)}
    two = {p: ("second", 0, p) for p in range(4)}
    seq += [("compute", 0, last - 1), ("compute", 0, last), ("gain", 0, 0)]
    seq += [term[0], ("gain_a", 0, 0), term[1]] + far[0] + [term[2]] + far[1]
    seq += [one[0], term[3]] + far[2] + far[3] + [("gain_x", 0, 0), ("calm", 0, 0)]
    seq += [one[3], near[0], near[1], one[2], near[2], near[3], ("gain_z", 0, 0)]
    seq += near[4:6] + [one[1]] + near[6:] + [("rs_end", 0, k) for k in range(NCH)]
    seq += [two[0], two[3], ("gain_end", 0, 0), ("drain", 0, 0), two[1], two[2]]
    return seq


def kernel(
    X, Z, Y, s,
    x_hbm, d_hbm, gain_hbm, wu_hbm, wd_hbm, counts_hbm,
    dtok_out, dup_out, ddn_out, dgain_out,
    dtok_ref, dup_ref, ddn_ref, dgain_ref,
    counts_ref, gain_ref, B, wu, wd, wg, wgT, gainb, Q, Qs, RSs, RSr, U, V, Gs, Xr, Ss, Zr, Gz, Zf, Sx, Xf,
    DH, CT, g1, g1r, g2, gy, g3, gx, g4, gz, live_s,
    loc, out_s, ag_s, ag_r, sb_s, sb_r, qs_s, qs_r, rs_s, rs_r, x_s, x_r, z_s, z_r,
    ga_s, ga_r, gy_s, gy_r, gx_s, gx_r, gz_s, gz_r, told,
):
    r = lax.axis_index("region")
    m = lax.axis_index("mp")
    x, z = r // Z, r % Z
    y, c = m // 2, m % 2
    H2 = Y // 2
    TC = B.shape[3]
    FB = B.shape[2] // 2
    D = wu.shape[0]
    FH = wu.shape[1]
    sib = (r, y * 2 + 1 - c)

    def ydev(k):
        return (r, ((y + k + Y) % Y) * 2 + c)

    def xdev(k):
        return (((x + k + X) % X) * Z + z, m)

    def zdev(k):
        return (x * Z + (z + k + Z) % Z, m)

    bar = pltpu.get_barrier_semaphore()
    sides = [(ydev(1), 1, H2), (ydev(-1), 0, H2), (xdev(1), 3, X // 2), (xdev(-1), 2, X // 2)]

    def greet(p):
        pl.semaphore_signal(bar, 1, device_id=p, device_id_type=MESH)

    half = Z // 2
    low = z < half
    base = z - z % half

    def zmate(k):
        return (x * Z + base + (z + k) % half, m)

    def zacross(k):
        return (x * Z + half - base + k, m)

    for p in [sib, ydev(1), ydev(-1), xdev(1), xdev(-1)] + [zmate(k) for k in range(1, half)]:
        greet(p)

    own = []
    for k in range(NCH):
        lanes = pl.ds(k * TC, TC)
        own.append(pltpu.make_async_copy(x_hbm.at[:, lanes], B.at[k, m, pl.ds(0, FB)], loc.at[2 * k]))
        own.append(pltpu.make_async_copy(d_hbm.at[:, lanes], B.at[k, m, pl.ds(FB, FB)], loc.at[2 * k + 1]))
    wcp = [
        pltpu.make_async_copy(wu_hbm, wu, loc.at[2 * NCH]),
        pltpu.make_async_copy(wd_hbm, wd, loc.at[2 * NCH + 1]),
        pltpu.make_async_copy(gain_hbm, gain_ref, loc.at[2 * NCH + 2]),
        pltpu.make_async_copy(counts_hbm, counts_ref, loc.at[2 * NCH + 3]),
    ]
    for cp in own + wcp:
        cp.start()
    wcp[3].wait()
    load = counts_ref[0] + counts_ref[1] + counts_ref[2] + counts_ref[3]
    for k in range(NCH):
        at = lax.broadcasted_iota(jnp.int32, (1, TC), 1) + k * TC
        live_s[k] = jnp.where(at < load, 1.0, 0.0).astype(F32)
    for cp in own:
        cp.wait()
    pl.when(low)(lambda: pl.semaphore_wait(bar, 4 + half))
    pl.when(z >= half)(lambda: pl.semaphore_wait(bar, 4 + 2 * half))
    for k in range(half):
        greet(zacross(k))

    pending = []

    def hear(n):
        for i in range(4):
            if sides[i][2] > n > 0:
                pl.semaphore_wait(told.at[i], 1)

    def upper_in():
        pl.when(low)(lambda: pl.semaphore_wait(bar, half))

    def tell(n):
        hear(n - 1)
        for peer, i, far in sides:
            if far > n:
                pl.semaphore_signal(told.at[i], 1, device_id=peer, device_id_type=MESH)

    given = []

    def give(src, dst):
        cp = pltpu.make_async_copy(src, dst, out_s.at[len(given)])
        cp.start()
        given.append(cp)

    def remote(src, dst, ss, rs, dev):
        return pltpu.make_async_remote_copy(
            src_ref=src, dst_ref=dst, send_sem=ss, recv_sem=rs, device_id=dev, device_id_type=MESH
        )

    def go(cp):
        cp.start()
        pending.append(cp)

    def ag(d, h, k):
        sg = 1 if d == 0 else -1
        slot = ((y - sg * (h - 1) + Y) % Y) * 2 + c
        ref = B.at[k, slot] if h < H2 else B.at[k, slot, pl.ds(d * FB, FB)]
        return remote(ref, ref, ag_s.at[d, h - 1, k], ag_r.at[d, h - 1, k], ydev(sg))

    def sb(j, k):
        ref = B.at[k, ((y + j + Y) % Y) * 2 + c]
        return remote(ref, ref, sb_s.at[j % Y, k], sb_r.at[j % Y, k], sib)

    def own_send(k):
        go(ag(0, 1, k))
        go(ag(1, 1, k))
        go(sb(0, k))

    def arrive(h, k):
        for d in range(2):
            sg = 1 if d == 0 else -1
            ag(d, h, k).wait_recv()
            if h < H2:
                go(ag(d, h + 1, k))
                go(sb(-sg * h, k))
        if h == H2:
            go(sb(H2, k))

    def prep():
        wcp[2].wait()
        gb = jnp.broadcast_to(gain_ref[...], (128, D)).T
        gainb[...] = gb.reshape(gainb.shape)
        wcp[0].wait()
        for j in range(FH // 128):
            t = wu[:, pl.ds(j * 128, 128)].astype(F32) * gb
            wg[:, pl.ds(j * 128, 128)] = t.astype(BF16)
            wgT[pl.ds(j * 128, 128), :] = t.T.astype(BF16)
        wcp[1].wait()

    def compute(k):
        for j in range(Y):
            sb(j, k).wait_recv()
        last = k == NCH - 1
        xc = B[k, :, 0:FB, :].reshape(D, TC)
        dc = B[k, :, FB : 2 * FB, :].reshape(D, TC)
        xf = xc.astype(F32)
        inv = lax.rsqrt(jnp.sum(xf * xf, axis=0, keepdims=True) * (1.0 / D) + EPSILON)
        live = live_s[k]
        v = nn_dot(wgT[...], xc) * inv
        a = nn_dot(wd[...], dc)
        v2 = v * v
        t = jnp.tanh(GC * v * (1.0 + 0.044715 * v2))
        cdf = 0.5 + 0.5 * t
        act = (v * cdf * live).astype(BF16)
        gp = cdf + (0.5 * GC) * v * (1.0 - t * t) * (1.0 + (3 * 0.044715) * v2)
        dh = a * gp * (live * inv)
        ct = jnp.sum(dh * v, axis=0, keepdims=True) * inv * (1.0 / D)
        dhb = dh.astype(BF16)

        def grads(u, lhs, rhs, acc):
            term = nt_dot(lhs, rhs)
            if k > 0:
                term = acc[...] + term
            acc[...] = term
            if last:
                for p in (2 * u + 1, 2 * u):
                    half = term[:, (p % 2) * HF : (p % 2) * HF + HF].astype(BF16)
                    half = half.reshape(X, Z, -1, HF)
                    if p in ZFIRST:
                        for i in range(X):
                            for j in range(Z):
                                Gz[p, j, i] = half[i, j]
                        for i in range(1, Z):
                            go(z_first(p, i))
                    else:
                        Gs[p] = half
                        for i in range(1, X):
                            go(xstage(p, i))

        grads(0, xc, dhb, U)
        grads(1, dc, act, V)
        DH[k] = dhb
        CT[k] = ct

    def gain_start():
        wuu = (wu[...].astype(F32) * U[...]).astype(BF16)
        gv = nt_dot(jnp.ones((8, FH), BF16), wuu)
        for j in range(Y):
            g1[j] = gv[:, j * 128 : (j + 1) * 128]
        go(gacopy())

    def terms(k):
        q = nn_dot(wg[...], DH[k]) - B[k, :, 0:FB, :].reshape(D, TC).astype(F32) * CT[k]
        q = q.astype(BF16)
        for j in range(2 * Y):
            Q[k, j % 2, j // 2] = q[j * FB : (j + 1) * FB, :]
        go(qcopy(k))

    def qcopy(k):
        return remote(Q.at[k, 1 - c], Qs.at[k], qs_s.at[k], qs_r.at[k], sib)

    def gacopy():
        return remote(g1, g1r, ga_s, ga_r, sib)

    def xstage(p, i):
        return remote(
            Gs.at[p, (x + i) % X], Xr.at[p, i - 1], x_s.at[p, i - 1], x_r.at[p, i - 1], xdev(i)
        )

    def zstage(p, i):
        return remote(
            Ss.at[p, (z + i) % Z], Zr.at[p, i - 1], z_s.at[p, i - 1], z_r.at[p, i - 1], zdev(i)
        )

    def z_first(p, i):
        return remote(
            Gz.at[p, (z + i) % Z], Zf.at[p, i - 1], z_s.at[p, i - 1], z_r.at[p, i - 1], zdev(i)
        )

    def x_second(p, i):
        return remote(
            Sx.at[p, (x + i) % X], Xf.at[p, i - 1], x_s.at[p, i - 1], x_r.at[p, i - 1], xdev(i)
        )

    def rs(d, h, k):
        sg = 1 if d == 0 else -1
        if h < H2:
            src, dst = RSs.at[d, h - 1, k], RSr.at[d, h - 1, k]
        else:
            sg = 2 * sg
            src = RSs.at[d, h - 1, k, pl.ds(0, FB // 2)]
            dst = RSr.at[d, h - 1, k, pl.ds(0, FB // 2)]
        return remote(src, dst, rs_s.at[d, h - 1, k], rs_r.at[d, h - 1, k], ydev(sg))

    def came(d, h, k):
        rs(d, h, k).wait_recv()
        if h < H2:
            return RSr[d, h - 1, k].astype(F32)
        half = RSr[d, h - 1, k, 0 : FB // 2, :].astype(F32)
        zero = jnp.zeros_like(half)
        return jnp.concatenate([half, zero] if d == 0 else [zero, half], axis=0)

    def both(ty, k):
        return Q[k, c, ty].astype(F32) + Qs[k, ty].astype(F32)

    def rs_step(h, k):
        if h == H2:
            qcopy(k).wait_recv()
            p = both((y + H2) % Y, k).astype(BF16)
            RSs[0, h - 1, k, 0 : FB // 2, :] = p[0 : FB // 2, :]
            RSs[1, h - 1, k, 0 : FB // 2, :] = p[FB // 2 :, :]
            for d in range(2):
                go(rs(d, h, k))
            return
        for d in range(2):
            sg = 1 if d == 0 else -1
            p = both((y + sg * h + Y) % Y, k)
            if h < H2 - 1:
                p = p + came(d, h + 1, k)
            if h == H2 - 2:
                p = p + came(d, H2, k)
            RSs[d, h - 1, k] = p.astype(BF16)
            go(rs(d, h, k))

    def rs_end(k):
        tot = both(y, k) + came(0, 1, k) + came(1, 1, k)
        tot = B[k, m, FB : 2 * FB, :].astype(F32) + tot
        lanes = pl.ds(k * TC, TC)
        dtok_ref[:, lanes] = (tot * live_s[k]).astype(BF16)
        give(dtok_ref.at[:, lanes], dtok_out.at[:, lanes])

    def gain_a():
        gacopy().wait_recv()
        g2[...] = g1[...] + g1r[...]
        for i in range(1, Y):
            go(gycopy(i))

    def gycopy(i):
        return remote(g2.at[(y + i) % Y], gy.at[i - 1], gy_s.at[i - 1], gy_r.at[i - 1], ydev(i))

    def gxcopy(i):
        return remote(g3, gx.at[i - 1], gx_s.at[i - 1], gx_r.at[i - 1], xdev(i))

    def gzcopy(i):
        return remote(g4, gz.at[i - 1], gz_s.at[i - 1], gz_r.at[i - 1], zdev(i))

    def gain_x():
        t = g2[y]
        for i in range(1, Y):
            gycopy(i).wait_recv()
            t = t + gy[i - 1]
        g3[...] = t
        for i in range(1, X):
            go(gxcopy(i))

    def gain_z():
        t = g3[...]
        for i in range(1, X):
            gxcopy(i).wait_recv()
            t = t + gx[i - 1]
        g4[...] = t
        for i in range(1, Z):
            go(gzcopy(i))

    def gain_end():
        t = g4[...]
        for i in range(1, Z):
            gzcopy(i).wait_recv()
            t = t + gz[i - 1]
        t = t * s
        dgain_ref[...] = jnp.where(c == 0, t[0:1, 0:FB], t[0:1, FB : 2 * FB])
        give(dgain_ref, dgain_out)

    def first_end(p):
        if p in ZFIRST:
            t = Gz[p, z].astype(F32)
            for i in range(1, Z):
                z_first(p, i).wait_recv()
                t = t + Zf[p, i - 1].astype(F32)
            Sx[p] = t.astype(BF16)
            for i in range(1, X):
                go(x_second(p, i))
        else:
            t = Gs[p, x].astype(F32)
            for i in range(1, X):
                xstage(p, i).wait_recv()
                t = t + Xr[p, i - 1].astype(F32)
            Ss[p] = t.astype(BF16)
            for i in range(1, Z):
                go(zstage(p, i))

    def second_end(p):
        if p in ZFIRST:
            t = Sx[p, x].astype(F32)
            for i in range(1, X):
                x_second(p, i).wait_recv()
                t = t + Xf[p, i - 1].astype(F32)
        else:
            t = Ss[p, z].astype(F32)
            for i in range(1, Z):
                zstage(p, i).wait_recv()
                t = t + Zr[p, i - 1].astype(F32)
        t = t * s
        lanes = pl.ds((p % 2) * HF, HF)
        if p < 2:
            dup_ref[:, lanes] = t * gainb[r]
            give(dup_ref.at[:, lanes], dup_out.at[:, lanes])
        else:
            ddn_ref[:, lanes] = t
            give(ddn_ref.at[:, lanes], ddn_out.at[:, lanes])

    def calm():
        for _ in range(NCH * (4 * H2 - 1)):
            pending.pop(0).wait_send()

    def drain():
        while pending:
            pending.pop().wait_send()

    steps = {
        "own": lambda h, k: own_send(k),
        "prep": lambda h, k: prep(),
        "arrive": arrive,
        "compute": lambda h, k: compute(k),
        "terms": lambda h, k: terms(k),
        "gain": lambda h, k: gain_start(),
        "rs": rs_step,
        "rs_end": lambda h, k: rs_end(k),
        "first": lambda h, k: first_end(k),
        "second": lambda h, k: second_end(k),
        "gain_a": lambda h, k: gain_a(),
        "gain_x": lambda h, k: gain_x(),
        "gain_z": lambda h, k: gain_z(),
        "gain_end": lambda h, k: gain_end(),
        "drain": lambda h, k: drain(),
        "calm": lambda h, k: calm(),
        "tell": lambda h, k: tell(h),
        "hear": lambda h, k: hear(h),
        "upper": lambda h, k: upper_in(),
    }
    for what, h, k in order_of(H2):
        steps[what](h, k)
    drain()
    for cp in given:
        cp.wait()


def hand_out(*refs):
    n = (len(refs) - 2) // 3
    into, out = refs[-2], refs[-1]
    loads = [pltpu.make_async_copy(refs[i], refs[2 * n + i], into.at[i]) for i in range(n)]
    stores = [pltpu.make_async_copy(refs[2 * n + i], refs[n + i], out.at[i]) for i in range(n)]
    for cp in loads:
        cp.start()
    for cp, st in zip(loads, stores):
        cp.wait()
        st.start()
    for st in stores:
        st.wait()


def solution(mesh):
    R, M = mesh.shape["region"], mesh.shape["mp"]
    X = max(k for k in (1, 2, 4) if k * k <= R)
    Z, Y = R // X, M // 2
    s = 1.0 / math.sqrt(BAL * R)

    def on_device(tokens, cotangent, gain, w_up, w_down, counts):
        T, FB = tokens.shape
        D, FH = w_up.shape
        TC = T // NCH
        RW = D // R
        H2 = Y // 2
        dma = pltpu.SemaphoreType.DMA
        shapes = [
            jax.ShapeDtypeStruct((FB, T), BF16),
            jax.ShapeDtypeStruct((RW, FH), F32),
            jax.ShapeDtypeStruct((RW, FH), F32),
            jax.ShapeDtypeStruct((1, FB), F32),
        ]
        scratch = [pltpu.VMEM(t.shape, t.dtype) for t in shapes] + [
            pltpu.SMEM((4,), jnp.int32),
            pltpu.VMEM((1, D), F32),
            pltpu.VMEM((NCH, M, 2 * FB, TC), BF16),
            pltpu.VMEM((D, FH), BF16),
            pltpu.VMEM((FH, D), BF16),
            pltpu.VMEM((D, FH), BF16),
            pltpu.VMEM((FH, D), BF16),
            pltpu.VMEM((R, RW, 128), F32),
            pltpu.VMEM((NCH, 2, Y, FB, TC), BF16),
            pltpu.VMEM((NCH, Y, FB, TC), BF16),
            pltpu.VMEM((2, H2, NCH, FB, TC), BF16),
            pltpu.VMEM((2, H2, NCH, FB, TC), BF16),
            pltpu.VMEM((D, FH), F32),
            pltpu.VMEM((D, FH), F32),
            pltpu.VMEM((4, X, Z, RW, HF), BF16),
            pltpu.VMEM((4, X, Z, RW, HF), BF16),
            pltpu.VMEM((4, Z, RW, HF), BF16),
            pltpu.VMEM((4, Z, RW, HF), BF16),
            pltpu.VMEM((4, Z, X, RW, HF), BF16),
            pltpu.VMEM((4, Z, X, RW, HF), BF16),
            pltpu.VMEM((4, X, RW, HF), BF16),
            pltpu.VMEM((4, X, RW, HF), BF16),
            pltpu.VMEM((NCH, FH, TC), BF16),
            pltpu.VMEM((NCH, 1, TC), F32),
            pltpu.VMEM((Y, 8, 128), F32),
            pltpu.VMEM((Y, 8, 128), F32),
            pltpu.VMEM((Y, 8, 128), F32),
            pltpu.VMEM((Y, 8, 128), F32),
            pltpu.VMEM((8, 128), F32),
            pltpu.VMEM((X, 8, 128), F32),
            pltpu.VMEM((8, 128), F32),
            pltpu.VMEM((Z, 8, 128), F32),
            pltpu.VMEM((NCH, 1, TC), F32),
            dma((2 * NCH + 4,)),
            dma((NCH + 5,)),
            dma((2, H2, NCH)),
            dma((2, H2, NCH)),
            dma((Y, NCH)),
            dma((Y, NCH)),
            dma((NCH,)),
            dma((NCH,)),
            dma((2, H2, NCH)),
            dma((2, H2, NCH)),
            dma((4, X)),
            dma((4, X)),
            dma((4, Z)),
            dma((4, Z)),
            dma,
            dma,
            dma((Y,)),
            dma((Y,)),
            dma((X,)),
            dma((X,)),
            dma((Z,)),
            dma((Z,)),
            pltpu.SemaphoreType.REGULAR((4,)),
        ]
        hbm = pl.BlockSpec(memory_space=pltpu.HBM)
        sums = pl.pallas_call(
            functools.partial(kernel, X, Z, Y, s),
            out_shape=shapes,
            in_specs=[hbm] * 6,
            out_specs=[hbm] * 4,
            scratch_shapes=scratch,
            compiler_params=pltpu.CompilerParams(
                collective_id=0, has_side_effects=True, vmem_limit_bytes=56 << 20
            ),
            cost_estimate=pl.CostEstimate(
                flops=10 * T * D * FH, bytes_accessed=4 << 20, transcendentals=T * FH
            ),
        )(tokens.T, cotangent.T, gain.reshape(1, D), w_up, w_down, counts)
        dtok, dup, ddn, dgain = pl.pallas_call(
            hand_out,
            out_shape=shapes,
            in_specs=[hbm] * 4,
            out_specs=[hbm] * 4,
            scratch_shapes=[pltpu.VMEM(t.shape, t.dtype) for t in shapes] + [dma((4,)), dma((4,))],
            compiler_params=pltpu.CompilerParams(vmem_limit_bytes=56 << 20),
        )(*sums)
        return dtok.T, dup, ddn.T, dgain.reshape(FB)

    return jax.shard_map(
        on_device,
        mesh=mesh,
        in_specs=(
            P("region", "mp"), P("region", "mp"), P(), P(None, "mp"), P("mp", None), P("region"),
        ),
        out_specs=(P("region", "mp"), P("region", "mp"), P("mp", "region"), P("mp")),
        check_vma=False,
    )
```

```python
import functools
import math

import jax
import jax.numpy as jnp
from jax import lax
from jax.experimental import pallas as pl
from jax.experimental.pallas import tpu as pltpu
from jax.sharding import PartitionSpec as P

BAL = 496
EPSILON = 1e-05
MESH = pl.DeviceIdType.MESH
F32 = jnp.float32
BF16 = jnp.bfloat16
NCH = 4
ZFIRST = (1,)
HF = 128
GC = math.sqrt(2.0 / math.pi)


def nt_dot(a, b):
    return lax.dot_general(a, b, (((1,), (1,)), ((), ())), preferred_element_type=F32)


def nn_dot(a, b):
    return lax.dot_general(a, b, (((1,), (0,)), ((), ())), preferred_element_type=F32)


def order_of(H2):
    last = NCH - 1
    seq = [("own", 0, k) for k in range(NCH)] + [("prep", 0, 0)]
    for h in range(1, H2):
        seq += [("tell", h - 1, 0)] if h > 1 else []
        seq += [("arrive", h, k) for k in range(NCH)]
    seq.append(("tell", H2 - 1, 0))
    for k in range(NCH):
        seq.append(("arrive", H2, k))
        if 1 <= k < last:
            seq.append(("compute", 0, k - 1))
    seq += [("hear", H2 - 1, 0), ("upper", 0, 0)]
    far = [[("rs", H2, k), ("rs", H2 - 1, k)] for k in range(NCH)]
    near = [("rs", h, k) for h in range(H2 - 2, 0, -1) for k in range(NCH)]
    term = [("terms", 0, k) for k in range(NCH)]
    one = {p: ("first", 0, p) for p in range(4)}
    two = {p: ("second", 0, p) for p in range(4)}
    seq += [("compute", 0, last - 1), ("compute", 0, last), ("gain", 0, 0)]
    seq += [term[0], ("gain_a", 0, 0), term[1]] + far[0] + [term[2]] + far[1]
    seq += [one[0], term[3]] + far[2] + far[3] + [("gain_x", 0, 0), ("calm", 0, 0)]
    seq += [one[3], near[0], near[1], one[2], near[2], near[3], ("gain_z", 0, 0)]
    seq += near[4:6] + [one[1]] + near[6:] + [("rs_end", 0, k) for k in range(NCH)]
    seq += [two[0], two[3], ("gain_end", 0, 0), ("drain", 0, 0), two[1], two[2]]
    return seq


def kernel(
    X, Z, Y, s,
    x_hbm, d_hbm, gain_hbm, wu_hbm, wd_hbm, counts_hbm,
    dtok_out, dup_out, ddn_out, dgain_out,
    dtok_ref, dup_ref, ddn_ref, dgain_ref,
    counts_ref, gain_ref, B, wu, wd, wg, wgT, gainb, Q, Qs, RSs, RSr, U, V, Gs, Xr, Ss, Zr, Gz, Zf, Sx, Xf,
    DH, CT, AC, g1, g1r, g2, gy, g3, gx, g4, gz, live_s,
    loc, out_s, ag_s, ag_r, sb_s, sb_r, qs_s, qs_r, rs_s, rs_r, x_s, x_r, z_s, z_r,
    ga_s, ga_r, gy_s, gy_r, gx_s, gx_r, gz_s, gz_r, told,
):
    r = lax.axis_index("region")
    m = lax.axis_index("mp")
    x, z = r // Z, r % Z
    y, c = m // 2, m % 2
    H2 = Y // 2
    TC = B.shape[3]
    FB = B.shape[2] // 2
    D = wu.shape[0]
    FH = wu.shape[1]
    sib = (r, y * 2 + 1 - c)

    def ydev(k):
        return (r, ((y + k + Y) % Y) * 2 + c)

    def xdev(k):
        return (((x + k + X) % X) * Z + z, m)

    def zdev(k):
        return (x * Z + (z + k + Z) % Z, m)

    bar = pltpu.get_barrier_semaphore()
    sides = [(ydev(1), 1, H2), (ydev(-1), 0, H2), (xdev(1), 3, X // 2), (xdev(-1), 2, X // 2)]

    def greet(p):
        pl.semaphore_signal(bar, 1, device_id=p, device_id_type=MESH)

    half = Z // 2
    low = z < half
    base = z - z % half

    def zmate(k):
        return (x * Z + base + (z + k) % half, m)

    def zacross(k):
        return (x * Z + half - base + k, m)

    for p in [sib, ydev(1), ydev(-1), xdev(1), xdev(-1)] + [zmate(k) for k in range(1, half)]:
        greet(p)

    own = []
    for k in range(NCH):
        lanes = pl.ds(k * TC, TC)
        own.append(pltpu.make_async_copy(x_hbm.at[:, lanes], B.at[k, m, pl.ds(0, FB)], loc.at[2 * k]))
        own.append(pltpu.make_async_copy(d_hbm.at[:, lanes], B.at[k, m, pl.ds(FB, FB)], loc.at[2 * k + 1]))
    wcp = [
        pltpu.make_async_copy(wu_hbm, wu, loc.at[2 * NCH]),
        pltpu.make_async_copy(wd_hbm, wd, loc.at[2 * NCH + 1]),
        pltpu.make_async_copy(gain_hbm, gain_ref, loc.at[2 * NCH + 2]),
        pltpu.make_async_copy(counts_hbm, counts_ref, loc.at[2 * NCH + 3]),
    ]
    for cp in own + wcp:
        cp.start()
    wcp[3].wait()
    load = counts_ref[0] + counts_ref[1] + counts_ref[2] + counts_ref[3]
    for k in range(NCH):
        at = lax.broadcasted_iota(jnp.int32, (1, TC), 1) + k * TC
        live_s[k] = jnp.where(at < load, 1.0, 0.0).astype(F32)
    for cp in own:
        cp.wait()
    pl.when(low)(lambda: pl.semaphore_wait(bar, 4 + half))
    pl.when(z >= half)(lambda: pl.semaphore_wait(bar, 4 + 2 * half))
    for k in range(half):
        greet(zacross(k))

    pending = []

    def hear(n):
        for i in range(4):
            if sides[i][2] > n > 0:
                pl.semaphore_wait(told.at[i], 1)

    def upper_in():
        pl.when(low)(lambda: pl.semaphore_wait(bar, half))

    def tell(n):
        hear(n - 1)
        for peer, i, far in sides:
            if far > n:
                pl.semaphore_signal(told.at[i], 1, device_id=peer, device_id_type=MESH)

    given = []

    def give(src, dst):
        cp = pltpu.make_async_copy(src, dst, out_s.at[len(given)])
        cp.start()
        given.append(cp)

    def remote(src, dst, ss, rs, dev):
        return pltpu.make_async_remote_copy(
            src_ref=src, dst_ref=dst, send_sem=ss, recv_sem=rs, device_id=dev, device_id_type=MESH
        )

    def go(cp):
        cp.start()
        pending.append(cp)

    def ag(d, h, k):
        sg = 1 if d == 0 else -1
        slot = ((y - sg * (h - 1) + Y) % Y) * 2 + c
        ref = B.at[k, slot] if h < H2 else B.at[k, slot, pl.ds(d * FB, FB)]
        return remote(ref, ref, ag_s.at[d, h - 1, k], ag_r.at[d, h - 1, k], ydev(sg))

    def sb(j, k):
        ref = B.at[k, ((y + j + Y) % Y) * 2 + c]
        return remote(ref, ref, sb_s.at[j % Y, k], sb_r.at[j % Y, k], sib)

    def own_send(k):
        go(ag(0, 1, k))
        go(ag(1, 1, k))
        go(sb(0, k))

    def arrive(h, k):
        for d in range(2):
            sg = 1 if d == 0 else -1
            ag(d, h, k).wait_recv()
            if h < H2:
                go(ag(d, h + 1, k))
                go(sb(-sg * h, k))
        if h == H2:
            go(sb(H2, k))

    def prep():
        wcp[2].wait()
        gb = jnp.broadcast_to(gain_ref[...], (128, D)).T
        gainb[...] = gb.reshape(gainb.shape)
        wcp[0].wait()
        for j in range(FH // 128):
            t = wu[:, pl.ds(j * 128, 128)].astype(F32) * gb
            wg[:, pl.ds(j * 128, 128)] = t.astype(BF16)
            wgT[pl.ds(j * 128, 128), :] = t.T.astype(BF16)
        wcp[1].wait()

    def compute(k):
        for j in range(Y):
            sb(j, k).wait_recv()
        last = k == NCH - 1
        xc = B[k, :, 0:FB, :].reshape(D, TC)
        dc = B[k, :, FB : 2 * FB, :].reshape(D, TC)
        xf = xc.astype(F32)
        inv = lax.rsqrt(jnp.sum(xf * xf, axis=0, keepdims=True) * (1.0 / D) + EPSILON)
        live = live_s[k]
        v = nn_dot(wgT[...], xc) * inv
        a = nn_dot(wd[...], dc)
        v2 = v * v
        t = jnp.tanh(GC * v * (1.0 + 0.044715 * v2))
        cdf = 0.5 + 0.5 * t
        act = (v * cdf * live).astype(BF16)
        gp = cdf + (0.5 * GC) * v * (1.0 - t * t) * (1.0 + (3 * 0.044715) * v2)
        dh = a * gp * (live * inv)
        ct = jnp.sum(dh * v, axis=0, keepdims=True) * inv * (1.0 / D)
        dhb = dh.astype(BF16)

        DH[k] = dhb
        CT[k] = ct
        AC[k] = act
        if k % 2 == 0:
            return

        def grads(u, rhs, acc):
            rows = pl.ds(u * FB, FB)
            term = nt_dot(B[k - 1, :, rows, :].reshape(D, TC), rhs[k - 1])
            term = term + nt_dot(B[k, :, rows, :].reshape(D, TC), rhs[k])
            if k > 1:
                term = acc[...] + term
            if not last or u == 0:
                acc[...] = term
            if last:
                for p in (2 * u + 1, 2 * u):
                    half = term[:, (p % 2) * HF : (p % 2) * HF + HF].astype(BF16)
                    half = half.reshape(X, Z, -1, HF)
                    if p in ZFIRST:
                        for i in range(X):
                            for j in range(Z):
                                Gz[p, j, i] = half[i, j]
                        for i in range(1, Z):
                            go(z_first(p, i))
                    else:
                        Gs[p] = half
                        for i in range(1, X):
                            go(xstage(p, i))

        grads(0, DH, U)
        grads(1, AC, V)

    def gain_start():
        wuu = (wu[...].astype(F32) * U[...]).astype(BF16)
        gv = nt_dot(jnp.ones((8, FH), BF16), wuu)
        for j in range(Y):
            g1[j] = gv[:, j * 128 : (j + 1) * 128]
        go(gacopy())

    def terms(k):
        q = nn_dot(wg[...], DH[k]) - B[k, :, 0:FB, :].reshape(D, TC).astype(F32) * CT[k]
        q = q.astype(BF16)
        for j in range(2 * Y):
            Q[k, j % 2, j // 2] = q[j * FB : (j + 1) * FB, :]
        go(qcopy(k))

    def qcopy(k):
        return remote(Q.at[k, 1 - c], Qs.at[k], qs_s.at[k], qs_r.at[k], sib)

    def gacopy():
        return remote(g1, g1r, ga_s, ga_r, sib)

    def xstage(p, i):
        return remote(
            Gs.at[p, (x + i) % X], Xr.at[p, i - 1], x_s.at[p, i - 1], x_r.at[p, i - 1], xdev(i)
        )

    def zstage(p, i):
        return remote(
            Ss.at[p, (z + i) % Z], Zr.at[p, i - 1], z_s.at[p, i - 1], z_r.at[p, i - 1], zdev(i)
        )

    def z_first(p, i):
        return remote(
            Gz.at[p, (z + i) % Z], Zf.at[p, i - 1], z_s.at[p, i - 1], z_r.at[p, i - 1], zdev(i)
        )

    def x_second(p, i):
        return remote(
            Sx.at[p, (x + i) % X], Xf.at[p, i - 1], x_s.at[p, i - 1], x_r.at[p, i - 1], xdev(i)
        )

    def rs(d, h, k):
        sg = 1 if d == 0 else -1
        if h < H2:
            src, dst = RSs.at[d, h - 1, k], RSr.at[d, h - 1, k]
        else:
            sg = 2 * sg
            src = RSs.at[d, h - 1, k, pl.ds(0, FB // 2)]
            dst = RSr.at[d, h - 1, k, pl.ds(0, FB // 2)]
        return remote(src, dst, rs_s.at[d, h - 1, k], rs_r.at[d, h - 1, k], ydev(sg))

    def came(d, h, k):
        rs(d, h, k).wait_recv()
        if h < H2:
            return RSr[d, h - 1, k].astype(F32)
        half = RSr[d, h - 1, k, 0 : FB // 2, :].astype(F32)
        zero = jnp.zeros_like(half)
        return jnp.concatenate([half, zero] if d == 0 else [zero, half], axis=0)

    def both(ty, k):
        return Q[k, c, ty].astype(F32) + Qs[k, ty].astype(F32)

    def rs_step(h, k):
        if h == H2:
            qcopy(k).wait_recv()
            p = both((y + H2) % Y, k).astype(BF16)
            RSs[0, h - 1, k, 0 : FB // 2, :] = p[0 : FB // 2, :]
            RSs[1, h - 1, k, 0 : FB // 2, :] = p[FB // 2 :, :]
            for d in range(2):
                go(rs(d, h, k))
            return
        for d in range(2):
            sg = 1 if d == 0 else -1
            p = both((y + sg * h + Y) % Y, k)
            if h < H2 - 1:
                p = p + came(d, h + 1, k)
            if h == H2 - 2:
                p = p + came(d, H2, k)
            RSs[d, h - 1, k] = p.astype(BF16)
            go(rs(d, h, k))

    def rs_end(k):
        tot = both(y, k) + came(0, 1, k) + came(1, 1, k)
        tot = B[k, m, FB : 2 * FB, :].astype(F32) + tot
        lanes = pl.ds(k * TC, TC)
        dtok_ref[:, lanes] = (tot * live_s[k]).astype(BF16)
        give(dtok_ref.at[:, lanes], dtok_out.at[:, lanes])

    def gain_a():
        gacopy().wait_recv()
        g2[...] = g1[...] + g1r[...]
        for i in range(1, Y):
            go(gycopy(i))

    def gycopy(i):
        return remote(g2.at[(y + i) % Y], gy.at[i - 1], gy_s.at[i - 1], gy_r.at[i - 1], ydev(i))

    def gxcopy(i):
        return remote(g3, gx.at[i - 1], gx_s.at[i - 1], gx_r.at[i - 1], xdev(i))

    def gzcopy(i):
        return remote(g4, gz.at[i - 1], gz_s.at[i - 1], gz_r.at[i - 1], zdev(i))

    def gain_x():
        t = g2[y]
        for i in range(1, Y):
            gycopy(i).wait_recv()
            t = t + gy[i - 1]
        g3[...] = t
        for i in range(1, X):
            go(gxcopy(i))

    def gain_z():
        t = g3[...]
        for i in range(1, X):
            gxcopy(i).wait_recv()
            t = t + gx[i - 1]
        g4[...] = t
        for i in range(1, Z):
            go(gzcopy(i))

    def gain_end():
        t = g4[...]
        for i in range(1, Z):
            gzcopy(i).wait_recv()
            t = t + gz[i - 1]
        t = t * s
        dgain_ref[...] = jnp.where(c == 0, t[0:1, 0:FB], t[0:1, FB : 2 * FB])
        give(dgain_ref, dgain_out)

    def first_end(p):
        if p in ZFIRST:
            t = Gz[p, z].astype(F32)
            for i in range(1, Z):
                z_first(p, i).wait_recv()
                t = t + Zf[p, i - 1].astype(F32)
            Sx[p] = t.astype(BF16)
            for i in range(1, X):
                go(x_second(p, i))
        else:
            t = Gs[p, x].astype(F32)
            for i in range(1, X):
                xstage(p, i).wait_recv()
                t = t + Xr[p, i - 1].astype(F32)
            Ss[p] = t.astype(BF16)
            for i in range(1, Z):
                go(zstage(p, i))

    def second_end(p):
        if p in ZFIRST:
            t = Sx[p, x].astype(F32)
            for i in range(1, X):
                x_second(p, i).wait_recv()
                t = t + Xf[p, i - 1].astype(F32)
        else:
            t = Ss[p, z].astype(F32)
            for i in range(1, Z):
                zstage(p, i).wait_recv()
                t = t + Zr[p, i - 1].astype(F32)
        t = t * s
        lanes = pl.ds((p % 2) * HF, HF)
        if p < 2:
            dup_ref[:, lanes] = t * gainb[r]
            give(dup_ref.at[:, lanes], dup_out.at[:, lanes])
        else:
            ddn_ref[:, lanes] = t
            give(ddn_ref.at[:, lanes], ddn_out.at[:, lanes])

    def calm():
        for _ in range(NCH * (4 * H2 - 1)):
            pending.pop(0).wait_send()

    def drain():
        while pending:
            pending.pop().wait_send()

    steps = {
        "own": lambda h, k: own_send(k),
        "prep": lambda h, k: prep(),
        "arrive": arrive,
        "compute": lambda h, k: compute(k),
        "terms": lambda h, k: terms(k),
        "gain": lambda h, k: gain_start(),
        "rs": rs_step,
        "rs_end": lambda h, k: rs_end(k),
        "first": lambda h, k: first_end(k),
        "second": lambda h, k: second_end(k),
        "gain_a": lambda h, k: gain_a(),
        "gain_x": lambda h, k: gain_x(),
        "gain_z": lambda h, k: gain_z(),
        "gain_end": lambda h, k: gain_end(),
        "drain": lambda h, k: drain(),
        "calm": lambda h, k: calm(),
        "tell": lambda h, k: tell(h),
        "hear": lambda h, k: hear(h),
        "upper": lambda h, k: upper_in(),
    }
    for what, h, k in order_of(H2):
        steps[what](h, k)
    drain()
    for cp in given:
        cp.wait()


def hand_out(*refs):
    n = (len(refs) - 2) // 3
    into, out = refs[-2], refs[-1]
    loads = [pltpu.make_async_copy(refs[i], refs[2 * n + i], into.at[i]) for i in range(n)]
    stores = [pltpu.make_async_copy(refs[2 * n + i], refs[n + i], out.at[i]) for i in range(n)]
    for cp in loads:
        cp.start()
    for cp, st in zip(loads, stores):
        cp.wait()
        st.start()
    for st in stores:
        st.wait()


def solution(mesh):
    R, M = mesh.shape["region"], mesh.shape["mp"]
    X = max(k for k in (1, 2, 4) if k * k <= R)
    Z, Y = R // X, M // 2
    s = 1.0 / math.sqrt(BAL * R)

    def on_device(tokens, cotangent, gain, w_up, w_down, counts):
        T, FB = tokens.shape
        D, FH = w_up.shape
        TC = T // NCH
        RW = D // R
        H2 = Y // 2
        dma = pltpu.SemaphoreType.DMA
        shapes = [
            jax.ShapeDtypeStruct((FB, T), BF16),
            jax.ShapeDtypeStruct((RW, FH), F32),
            jax.ShapeDtypeStruct((RW, FH), F32),
            jax.ShapeDtypeStruct((1, FB), F32),
        ]
        scratch = [pltpu.VMEM(t.shape, t.dtype) for t in shapes] + [
            pltpu.SMEM((4,), jnp.int32),
            pltpu.VMEM((1, D), F32),
            pltpu.VMEM((NCH, M, 2 * FB, TC), BF16),
            pltpu.VMEM((D, FH), BF16),
            pltpu.VMEM((FH, D), BF16),
            pltpu.VMEM((D, FH), BF16),
            pltpu.VMEM((FH, D), BF16),
            pltpu.VMEM((R, RW, 128), F32),
            pltpu.VMEM((NCH, 2, Y, FB, TC), BF16),
            pltpu.VMEM((NCH, Y, FB, TC), BF16),
            pltpu.VMEM((2, H2, NCH, FB, TC), BF16),
            pltpu.VMEM((2, H2, NCH, FB, TC), BF16),
            pltpu.VMEM((D, FH), F32),
            pltpu.VMEM((D, FH), F32),
            pltpu.VMEM((4, X, Z, RW, HF), BF16),
            pltpu.VMEM((4, X, Z, RW, HF), BF16),
            pltpu.VMEM((4, Z, RW, HF), BF16),
            pltpu.VMEM((4, Z, RW, HF), BF16),
            pltpu.VMEM((4, Z, X, RW, HF), BF16),
            pltpu.VMEM((4, Z, X, RW, HF), BF16),
            pltpu.VMEM((4, X, RW, HF), BF16),
            pltpu.VMEM((4, X, RW, HF), BF16),
            pltpu.VMEM((NCH, FH, TC), BF16),
            pltpu.VMEM((NCH, 1, TC), F32),
            pltpu.VMEM((NCH, FH, TC), BF16),
            pltpu.VMEM((Y, 8, 128), F32),
            pltpu.VMEM((Y, 8, 128), F32),
            pltpu.VMEM((Y, 8, 128), F32),
            pltpu.VMEM((Y, 8, 128), F32),
            pltpu.VMEM((8, 128), F32),
            pltpu.VMEM((X, 8, 128), F32),
            pltpu.VMEM((8, 128), F32),
            pltpu.VMEM((Z, 8, 128), F32),
            pltpu.VMEM((NCH, 1, TC), F32),
            dma((2 * NCH + 4,)),
            dma((NCH + 5,)),
            dma((2, H2, NCH)),
            dma((2, H2, NCH)),
            dma((Y, NCH)),
            dma((Y, NCH)),
            dma((NCH,)),
            dma((NCH,)),
            dma((2, H2, NCH)),
            dma((2, H2, NCH)),
            dma((4, X)),
            dma((4, X)),
            dma((4, Z)),
            dma((4, Z)),
            dma,
            dma,
            dma((Y,)),
            dma((Y,)),
            dma((X,)),
            dma((X,)),
            dma((Z,)),
            dma((Z,)),
            pltpu.SemaphoreType.REGULAR((4,)),
        ]
        hbm = pl.BlockSpec(memory_space=pltpu.HBM)
        sums = pl.pallas_call(
            functools.partial(kernel, X, Z, Y, s),
            out_shape=shapes,
            in_specs=[hbm] * 6,
            out_specs=[hbm] * 4,
            scratch_shapes=scratch,
            compiler_params=pltpu.CompilerParams(
                collective_id=0, has_side_effects=True, vmem_limit_bytes=56 << 20
            ),
            cost_estimate=pl.CostEstimate(
                flops=10 * T * D * FH, bytes_accessed=4 << 20, transcendentals=T * FH
            ),
        )(tokens.T, cotangent.T, gain.reshape(1, D), w_up, w_down, counts)
        dtok, dup, ddn, dgain = pl.pallas_call(
            hand_out,
            out_shape=shapes,
            in_specs=[hbm] * 4,
            out_specs=[hbm] * 4,
            scratch_shapes=[pltpu.VMEM(t.shape, t.dtype) for t in shapes] + [dma((4,)), dma((4,))],
            compiler_params=pltpu.CompilerParams(vmem_limit_bytes=56 << 20),
        )(*sums)
        return dtok.T, dup, ddn.T, dgain.reshape(FB)

    return jax.shard_map(
        on_device,
        mesh=mesh,
        in_specs=(
            P("region", "mp"), P("region", "mp"), P(), P(None, "mp"), P("mp", None), P("region"),
        ),
        out_specs=(P("region", "mp"), P("region", "mp"), P("mp", "region"), P("mp")),
        check_vma=False,
    )
```
